128 devices in a mesh: space: 128 (over z, y, x, core).
Axes of the slice: x: 4, y: 4, z: 4, core: 2. Of those that a mesh axis runs over, the one named last changes fastest.
Arguments:
- feats: bfloat16 [196608, 256], P('space'), may hold values from -24 to 24
- nbr_brick: int32 [27, 196608], P(None, 'space'), may hold values from 0 to 31, as said below
- nbr_row: int32 [27, 196608], P(None, 'space'), may hold values from 0 to 63
- nbr_valid: int32 [27, 196608], P(None, 'space'), may hold values 0 or 1
- dest: int32 [196608, 1], P('space'), may hold values from 0 to 127; in each aligned block of 1536 rows (0 to 1535, 1536 to 3071, ...) at most 16 rows name the same one
- conv_weight: bfloat16 [27, 256, 256], replicated, may hold values from -0.078125 to 0.078125
- cpe_linear: bfloat16 [256, 256], replicated, may hold values from -0.375 to 0.375
- cpe_gain: float32 [256], replicated, may hold values from 0.1 to 1.9
- cpe_shift: float32 [256], replicated, may hold values from -2.5 to 2.5
- norm1_gain: float32 [256], replicated, may hold values from 0.1 to 1.9
- norm1_shift: float32 [256], replicated, may hold values from -2.5 to 2.5
- qkv_weight: bfloat16 [256, 768], replicated, may hold values from -4 to 4
- proj_weight: bfloat16 [256, 256], replicated, may hold values from -0.375 to 0.375
- norm2_gain: float32 [256], replicated, may hold values from 0.1 to 1.9
- norm2_shift: float32 [256], replicated, may hold values from -2.5 to 2.5
- fc1_weight: bfloat16 [256, 1024], replicated, may hold values from -0.375 to 0.375
- fc2_weight: bfloat16 [1024, 256], replicated, may hold values from -0.1875 to 0.1875
Outputs:
- block_output: bfloat16 [196608, 256], P('space')
The draws below stay inside these ranges and needn't reach their ends.
Inputs may be any that keep to these rules, and one draw needn't show every extreme that they name: `dest`: the rows of one device name one owner at most 16 times; some device names some owner exactly 16 times. `nbr_brick`: for a row in the device's brick b (0 to 23) the value is b + 4 + d with d from -4 to 4; values below 4 name the lower device's last bricks, values from 28 the upper device's first bricks.
All inputs are finite; a program needn't handle non-finite values. No bound on the sum of `nbr_valid` on one device may be relied on, other than what follows from the above.
Results may differ from the reference program's by a relative error of at most 0.013.
The reference program's roundings to bfloat16 on the way count: a program that leaves them out, or rounds other values in their place, can miss the bound.
Values may be sent and summed in bfloat16 or wider, within the bound.
A program may use at most 128 MiB of HBM per device.

```python
import math
import jax
import jax.numpy as jnp
import numpy as np
from jax import lax

C = 256
HEADS = 16
HEAD = 16
FF = 1024
KOFF = 27
PATCH = 1024
BR = 64
HB = 4
B_DEV = 24
PATCH_DEV = 2
TOTAL = 196608
SLOTS = 2048
N_SPACE = 128


def draw_feats(key, part):
    key = jax.random.fold_in(key, 11)
    first_key, second_key, third_key = jax.random.split(key, 3)
    row_scale = jnp.exp(jax.random.uniform(first_key, (TOTAL, 1), jnp.float32, math.log(0.3), math.log(3.0)))
    column_scale = jnp.exp(jax.random.uniform(second_key, (1, C), jnp.float32, math.log(0.5), math.log(2.0)))
    base = jnp.clip(jax.random.normal(third_key, (TOTAL, C), jnp.float32), -4.0, 4.0)
    return (base * row_scale * column_scale).astype(jnp.bfloat16)


def draw_nbr_brick(key, part):
    key = jax.random.fold_in(key, 23)
    column = jnp.arange(TOTAL, dtype=jnp.int32)
    local_brick = column % (B_DEV * BR) // BR
    offset_draw = jax.random.randint(key, (KOFF, TOTAL), -HB, HB + 1, dtype=jnp.int32)
    return local_brick[None, :] + HB + offset_draw


def draw_qkv_weight(key, part):
    key = jax.random.fold_in(key, 37)
    first_key = jax.random.fold_in(key, 0)
    base = jnp.clip(jax.random.normal(first_key, (C, 3 * C), jnp.float32), -4.0, 4.0) * C ** (-0.5)
    return base.astype(jnp.bfloat16)


def touch_ends(values, stream_key, least, largest):
    dims = values.shape
    place = [jax.random.randint(jax.random.fold_in(stream_key, axis), (), 0, dims[axis]) for axis in range(len(dims))]
    values = values.at[tuple(place)].set(least)
    longest = dims.index(max(dims))
    place[longest] = (place[longest] + 1) % dims[longest]
    return values.at[tuple(place)].set(largest)


def shared_out(own_key, own, number, rows, amount, top, limit, slope):
    sequence = jax.random.permutation(own_key, amount)
    packed, usual = portions_of(amount, rows * top, limit, slope, True), portions_of(amount, rows * top, limit, slope, False)
    places = jnp.arange(amount)

    def named(lengths, turn):
        used = int((lengths > 0).sum())
        fixed = max(1, used // 4)
        passed = fixed + (places - fixed + turn * (used - fixed)) % max(1, amount - fixed)
        return jnp.zeros((amount,), jnp.int32).at[sequence[jnp.where(places < fixed, places, passed)]].set(jnp.asarray(lengths, jnp.int32))

    lengths = jnp.where(number % 4 == 0, named(packed, number // 4), named(usual, number - number // 4 - 1))
    mixed = jax.random.permutation(jax.random.fold_in(own, 3), amount)
    giver, sink = mixed[0:amount // 2 * 2:2], mixed[1:amount // 2 * 2:2]
    slack = jnp.minimum(lengths[giver] - 1, limit - lengths[sink]) // 2
    slack = jnp.where((giver == sequence[0]) | (sink == sequence[0]) | (lengths[sink] == 0), 0, jnp.maximum(slack, 0))
    passed = jax.random.randint(jax.random.fold_in(own, 4), (amount // 2,), 0, 1 << 20) % (slack + 1)
    lengths = lengths.at[giver].add(-passed).at[sink].add(passed)
    items = jnp.searchsorted(jnp.cumsum(lengths), jnp.arange(rows * top), side="right").astype(jnp.int32)
    listing = items.reshape(top, rows).T
    listing = listing[jax.random.permutation(jax.random.fold_in(own, 1), rows)]
    turn = jax.random.randint(jax.random.fold_in(own, 2), (rows, 1), 0, top)
    return jnp.take_along_axis(listing, (jnp.arange(top)[None, :] + turn) % top, axis=1)


def portions_of(number_of, total, most, lean, full):
    portions = [(1 << 20) // math.isqrt(grade ** lean) + 1 for grade in range(1, number_of + 1)]
    largest = most if full else min(most, max(-(-total // number_of), total * portions[0] // sum(portions)))
    least = 1 if total - largest >= number_of - 1 else 0
    given, surplus = [largest] + [least] * (number_of - 1), total - largest - least * (number_of - 1)
    while surplus > 0:
        movable = [i for i in range(1, number_of) if given[i] < largest] or [i for i in range(1, number_of) if given[i] < most]
        pool, remaining = sum([portions[i] for i in movable]), surplus
        for i in movable:
            addition = min(most - given[i], max(1, remaining * portions[i] // pool), surplus)
            given[i] = given[i] + addition
            surplus = surplus - addition
    return np.array(given)


def normal_values(stream_key, dims, scale, limit, held_as=jnp.bfloat16):
    entries = scale * jax.random.normal(stream_key, dims, jnp.float32)
    return jnp.clip(entries, min=-limit, max=limit).astype(held_as)


def setup_inputs(seed: int = 0) -> dict:
    key_list = jax.random.split(jax.random.key(seed), 18)
    feats = draw_feats(jax.random.fold_in(key_list[17], 71), 0)
    nbr_brick = draw_nbr_brick(jax.random.fold_in(key_list[17], 71), 0)
    nbr_row = touch_ends(jax.random.randint(key_list[2], (KOFF, TOTAL), 0, BR), jax.random.fold_in(key_list[2], 1), 0, BR - 1).astype(jnp.int32)
    nbr_valid = touch_ends((jax.random.randint(key_list[3], (KOFF, TOTAL), 0, 4) < 3).astype(jnp.int32), jax.random.fold_in(key_list[3], 1), 0, 1)
    dest_keys = jax.random.split(jax.random.fold_in(key_list[4], 1), TOTAL // (B_DEV * BR))
    dest_turns = jax.random.permutation(jax.random.fold_in(key_list[4], 3), TOTAL // (B_DEV * BR))
    dest = jax.vmap(lambda own, number: shared_out(jax.random.fold_in(key_list[4], 2), own, number, B_DEV * BR, N_SPACE, 1, PATCH_DEV * PATCH // N_SPACE, 2))(dest_keys, dest_turns).reshape((TOTAL, 1))
    conv_weight = normal_values(key_list[5], (KOFF, C, C), (KOFF * C) ** -0.5, 0.078125)
    cpe_linear = normal_values(key_list[6], (C, C), C ** -0.5, 0.375)
    cpe_gain = jnp.clip(1.0 + 0.18 * jax.random.normal(key_list[7], (C,), jnp.float32), 0.1, 1.9)
    cpe_shift = normal_values(key_list[8], (C,), 0.5, 2.5, jnp.float32)
    norm1_gain = jnp.clip(1.0 + 0.18 * jax.random.normal(key_list[9], (C,), jnp.float32), 0.1, 1.9)
    norm1_shift = normal_values(key_list[10], (C,), 0.5, 2.5, jnp.float32)
    qkv_weight = draw_qkv_weight(jax.random.fold_in(key_list[17], 71), 0)
    proj_weight = normal_values(key_list[12], (C, C), C ** -0.5, 0.375)
    norm2_gain = jnp.clip(1.0 + 0.18 * jax.random.normal(key_list[13], (C,), jnp.float32), 0.1, 1.9)
    norm2_shift = normal_values(key_list[14], (C,), 0.5, 2.5, jnp.float32)
    fc1_weight = normal_values(key_list[15], (C, FF), C ** -0.5, 0.375)
    fc2_weight = normal_values(key_list[16], (FF, C), FF ** -0.5, 0.1875)
    return {"feats": feats, "nbr_brick": nbr_brick, "nbr_row": nbr_row, "nbr_valid": nbr_valid, "dest": dest, "conv_weight": conv_weight, "cpe_linear": cpe_linear, "cpe_gain": cpe_gain, "cpe_shift": cpe_shift, "norm1_gain": norm1_gain, "norm1_shift": norm1_shift, "qkv_weight": qkv_weight, "proj_weight": proj_weight, "norm2_gain": norm2_gain, "norm2_shift": norm2_shift, "fc1_weight": fc1_weight, "fc2_weight": fc2_weight}


def layer_norm(values, norm_gain, norm_shift):
    average = lax.optimization_barrier(jnp.mean(values, axis=-1, keepdims=True))
    centred = values - average
    spread = lax.optimization_barrier(jnp.mean(centred * centred, axis=-1, keepdims=True))
    return centred * lax.rsqrt(spread + 1e-05) * norm_gain + norm_shift

def attend(queries, keys, values, occupied):
    slot_count = queries.shape[0]
    patches = slot_count // PATCH
    groups = HEADS // 4

    def arrange(table):
        shaped = table.reshape(patches, PATCH, groups, 4, HEAD).transpose(0, 2, 1, 3, 4)
        return shaped.reshape(patches * groups, PATCH, 4, HEAD)
    masks = jnp.repeat(occupied.reshape(patches, PATCH), groups, axis=0)

    def one_group(items):
        query_part, key_part, value_part, mask_part = items
        scores = jnp.einsum('qhd,khd->hqk', query_part.astype(jnp.float32), key_part.astype(jnp.float32)) * HEAD ** (-0.5)
        scores = jnp.where(mask_part[None, None, :] > 0, scores, -1e+30)
        highest = lax.optimization_barrier(jnp.max(scores, axis=-1, keepdims=True))
        weights = jnp.exp(scores - highest)
        probable = (weights / lax.optimization_barrier(jnp.sum(weights, axis=-1, keepdims=True))).astype(jnp.bfloat16)
        mixed = jnp.einsum('hqk,khd->qhd', probable.astype(jnp.float32), value_part.astype(jnp.float32))
        return mixed.astype(jnp.bfloat16)
    mixed = lax.map(one_group, (arrange(queries), arrange(keys), arrange(values), masks))
    mixed = mixed.reshape(patches, groups, PATCH, 4, HEAD).transpose(0, 2, 1, 3, 4)
    return mixed.reshape(slot_count, HEADS * HEAD)

def reference(feats, nbr_brick, nbr_row, nbr_valid, dest, conv_weight, cpe_linear, cpe_gain, cpe_shift, norm1_gain, norm1_shift, qkv_weight, proj_weight, norm2_gain, norm2_shift, fc1_weight, fc2_weight):
    total_rows = feats.shape[0]
    device = jnp.arange(total_rows, dtype=jnp.int32) // (B_DEV * BR)

    def conv_step(carry, items):
        bricks, rows_in, valid, weight = items
        global_row = (device * B_DEV + bricks - HB) * BR + rows_in
        counted = (valid > 0) & (global_row >= 0) & (global_row < total_rows)
        picked = jnp.where(counted[:, None], feats[jnp.clip(global_row, 0, total_rows - 1)], jnp.zeros((), feats.dtype))
        return (carry + jnp.dot(picked, weight, preferred_element_type=jnp.float32), None)
    summed, _ = lax.scan(conv_step, jnp.zeros((total_rows, C), jnp.float32), (nbr_brick, nbr_row, nbr_valid, conv_weight))
    convolved = summed.astype(jnp.bfloat16)
    projected = jnp.dot(convolved, cpe_linear, preferred_element_type=jnp.float32)
    enriched = (feats.astype(jnp.float32) + layer_norm(projected, cpe_gain, cpe_shift)).astype(jnp.bfloat16)
    target = dest[:, 0].astype(jnp.int32)
    bin_key = (device * N_SPACE + target).astype(jnp.int32)
    order = jnp.argsort(bin_key, stable=True).astype(jnp.int32)
    counts = jnp.zeros((N_SPACE * N_SPACE,), jnp.int32).at[bin_key].add(1)
    starts = jnp.cumsum(counts).astype(jnp.int32) - counts
    sorted_key = bin_key[order]
    sorted_slot = jnp.arange(total_rows, dtype=jnp.int32) - starts[sorted_key]
    slot = jnp.zeros((total_rows,), jnp.int32).at[order].set(sorted_slot)
    where_placed = (target * SLOTS + slot * N_SPACE + device).astype(jnp.int32)
    placed = jnp.zeros((N_SPACE * SLOTS, C), jnp.bfloat16).at[where_placed].set(enriched)
    occupied = jnp.zeros((N_SPACE * SLOTS,), jnp.int32).at[where_placed].set(1)
    normed = layer_norm(placed.astype(jnp.float32), norm1_gain, norm1_shift).astype(jnp.bfloat16)
    qkv = jnp.dot(normed, qkv_weight, preferred_element_type=jnp.float32).astype(jnp.bfloat16)
    mixed = attend(qkv[:, :C], qkv[:, C:2 * C], qkv[:, 2 * C:], occupied)
    attended = jnp.dot(mixed, proj_weight, preferred_element_type=jnp.float32).astype(jnp.bfloat16)
    residual = enriched.astype(jnp.float32) + attended[where_placed].astype(jnp.float32)
    normed_two = layer_norm(residual, norm2_gain, norm2_shift).astype(jnp.bfloat16)
    hidden = jax.nn.gelu(jnp.dot(normed_two, fc1_weight, preferred_element_type=jnp.float32), approximate=False).astype(jnp.bfloat16)
    return (residual + jnp.dot(hidden, fc2_weight, preferred_element_type=jnp.float32)).astype(jnp.bfloat16)
```

```python
import functools

import jax
import jax.numpy as jnp
from jax import lax
from jax.experimental import pallas as pl
from jax.experimental.pallas import tpu as pltpu
from jax.sharding import PartitionSpec as P

HEADS = 16
HEAD = 16
C = 256
PATCH = 1024
BR = 64
HB = 4
KOFF = 27
ROWS = 1536
GROUP = 256
WINDOW = 768
LOG2E = 1.4426950408889634
SAFE_SCORE = 60.0
EMPTY = 1024.0
F32 = jnp.float32
BF16 = jnp.bfloat16


def layer_norm(values, gain, shift):
    average = jnp.mean(values, axis=-1, keepdims=True)
    centred = values - average
    spread = jnp.mean(centred * centred, axis=-1, keepdims=True)
    return centred * lax.rsqrt(spread + 1e-05) * gain + shift


def to_wire(rows):
    shaped = rows.reshape(128, 8, C)
    return jnp.concatenate([shaped[:, :, :128], shaped[:, :, 128:]], axis=1).astype(BF16)


def from_wire(block):
    wide = block.astype(F32)
    return jnp.concatenate([wide[:, :8], wide[:, 8:]], axis=2).reshape(PATCH, C)


def encode_kernel(
    ext, brick, row, valid, dest, weight, linear, gain, shift,
    enriched, out0, out1, position,
    ext_t, weight_t, relative, picked,
):
    for i in range(8):
        ext_t[:, GROUP * i : GROUP * (i + 1)] = ext[GROUP * i : GROUP * (i + 1), :].T

    def turn_weight(k, carry):
        weight_t[:, pl.ds(pl.multiple_of(k * C, C), C)] = weight[k].T
        return carry

    lax.fori_loop(0, KOFF, turn_weight, 0)
    base = lax.broadcasted_iota(jnp.int32, (KOFF, ROWS), 1) // GROUP * GROUP
    relative[...] = jnp.where(valid[...] > 0, brick[...] * BR + row[...] - base, -1)
    place = lax.broadcasted_iota(jnp.int32, (WINDOW, 1), 0)

    def conv_group(g, carry):
        columns = pl.ds(pl.multiple_of(g * GROUP, GROUP), GROUP)
        window = ext_t[:, pl.ds(pl.multiple_of(g * GROUP, GROUP), WINDOW)]
        for k in range(KOFF):
            chosen = jnp.where(relative[k : k + 1, columns] == place, 1.0, 0.0).astype(BF16)
            picked[C * k : C * (k + 1), :] = jnp.dot(
                window, chosen, preferred_element_type=F32
            ).astype(BF16)
        summed = jnp.dot(weight_t[...], picked[...], preferred_element_type=F32)
        convolved = summed.astype(BF16).T
        projected = jnp.dot(convolved, linear[...], preferred_element_type=F32)
        own = ext[pl.ds(pl.multiple_of((g + 1) * GROUP, GROUP), GROUP), :].astype(F32)
        enriched[columns, :] = (own + layer_norm(projected, gain[...], shift[...])).astype(BF16)
        return carry

    lax.fori_loop(0, ROWS // GROUP, conv_group, 0)

    owner = lax.broadcasted_iota(jnp.int32, (128, 1), 0)
    before = jnp.where(
        lax.broadcasted_iota(jnp.int32, (GROUP, GROUP), 0)
        < lax.broadcasted_iota(jnp.int32, (GROUP, GROUP), 1), 1.0, 0.0,
    ).astype(BF16)
    count = jnp.zeros((128, 1), F32)
    for b in range(ROWS // GROUP):
        part = slice(GROUP * b, GROUP * (b + 1))
        target = dest[0:1, part]
        named = jnp.where(target == owner, 1.0, 0.0)
        running = jnp.dot(named.astype(BF16), before, preferred_element_type=F32) + count
        slot = jnp.sum(running * named, axis=0, keepdims=True).astype(jnp.int32)
        count = count + jnp.sum(named, axis=1, keepdims=True)
        position[0:1, part] = jnp.where(slot < 8, 0, PATCH) + target * 8 + slot % 8

    counts = jnp.broadcast_to(count, (128, 128)).astype(BF16)
    expand = jnp.where(
        lax.broadcasted_iota(jnp.int32, (PATCH, 128), 0) // 8
        == lax.broadcasted_iota(jnp.int32, (PATCH, 128), 1), 1.0, 0.0,
    ).astype(BF16)
    filled = jnp.dot(expand, counts, preferred_element_type=F32)
    filled = jnp.concatenate([filled, filled], axis=1)
    slots = (lax.broadcasted_iota(jnp.int32, (PATCH, C), 0) % 8).astype(F32)
    where_to = position[...]
    for patch, out in enumerate((out0, out1)):
        index = lax.broadcasted_iota(jnp.int32, (PATCH, 1), 0) + patch * PATCH
        chosen = jnp.where(index == where_to, 1.0, 0.0).astype(BF16)
        moved = jnp.dot(chosen, enriched[...], preferred_element_type=F32)
        out[...] = to_wire(jnp.where(slots + 8.0 * patch < filled, moved, EMPTY))


def attend_kernel(
    arrived, gain, shift, qkv_weight, proj, attended,
    keys, query_t, value_t, mixed_t,
):
    rows = from_wire(arrived[...])
    occupied = rows[:, 0:1] < 0.5 * EMPTY
    rows = jnp.where(occupied, rows, 0.0)
    normed = layer_norm(rows, gain[...], shift[...]).astype(BF16)
    qkv = jnp.dot(normed, qkv_weight[...], preferred_element_type=F32).astype(BF16)
    queries = qkv[:, :C]
    keys[...] = qkv[:, C : 2 * C]
    values = jnp.where(occupied, qkv[:, 2 * C :], BF16(0))
    ones = jnp.broadcast_to(jnp.where(occupied, 1.0, 0.0), (PATCH, 128)).astype(BF16).T

    member = jnp.where(
        lax.broadcasted_iota(jnp.int32, (C, 128), 0) // HEAD
        == lax.broadcasted_iota(jnp.int32, (C, 128), 1), 1.0, 0.0,
    ).astype(BF16)

    def largest_square(table):
        wide = table.astype(F32)
        squares = jnp.dot((wide * wide).astype(BF16), member, preferred_element_type=F32)
        return jnp.max(squares, axis=0, keepdims=True)

    bound = jnp.max(largest_square(queries) * largest_square(qkv[:, C : 2 * C])) / HEAD
    safe = bound < SAFE_SCORE * SAFE_SCORE

    turned = (queries * BF16(HEAD ** (-0.5))).T
    values_t = values.T
    channel = lax.broadcasted_iota(jnp.int32, (128, 1), 0) // HEAD
    for h in range(HEADS):
        half, inside = h // 8, h % 8
        query_t[h] = jnp.where(channel == inside, turned[128 * half : 128 * (half + 1), :], BF16(0))
        value_t[h, :HEAD] = values_t[HEAD * h : HEAD * (h + 1), :]
        value_t[h, HEAD:] = ones[:HEAD, :]

    def finish(h, products, columns):
        below = products[HEAD : HEAD + 1, :]
        below = jnp.where(below > 0, below, 1.0)
        mixed_t[h, :, columns] = (products[:HEAD, :] / below).astype(BF16)

    block = 512

    @pl.when(safe)
    def _():
        def step(t, carry):
            half, column = t // (PATCH // block), t % (PATCH // block)
            columns = pl.ds(pl.multiple_of(column * block, block), block)
            some = keys[:, pl.ds(pl.multiple_of(half * 128, 128), 128)]
            for inside in range(8):
                h = half * 8 + inside
                scores = jnp.dot(some, query_t[h, :, columns], preferred_element_type=F32)
                weights = jnp.exp2(scores * LOG2E).astype(BF16)
                finish(h, jnp.dot(value_t[h], weights, preferred_element_type=F32), columns)
            return carry

        lax.fori_loop(0, 2 * (PATCH // block), step, 0)

    @pl.when(jnp.logical_not(safe))
    def _():
        penalty = jnp.where(occupied, 0.0, -1e30)

        def step(t, carry):
            h, column = t // (PATCH // 128), t % (PATCH // 128)
            columns = pl.ds(pl.multiple_of(column * 128, 128), 128)
            some = keys[:, pl.ds(pl.multiple_of(h // 8 * 128, 128), 128)]
            scores = jnp.dot(some, query_t[h, :, columns], preferred_element_type=F32)
            scores = jnp.where(penalty < 0.0, penalty, scores)
            highest = jnp.max(scores, axis=0, keepdims=True)
            weights = jnp.exp(scores - highest).astype(BF16)
            finish(h, jnp.dot(value_t[h], weights, preferred_element_type=F32), columns)
            return carry

        lax.fori_loop(0, HEADS * (PATCH // 128), step, 0)

    mixed = mixed_t[...].reshape(C, PATCH).T
    attended[...] = to_wire(jnp.dot(mixed, proj[...], preferred_element_type=F32))


def finish_kernel(
    returned0, returned1, enriched, position, gain, shift, fc1, fc2, output, returned_t
):
    for patch, block in enumerate((returned0, returned1)):
        returned_t[:, PATCH * patch : PATCH * (patch + 1)] = from_wire(block[...]).astype(BF16).T
    index = lax.broadcasted_iota(jnp.int32, (2 * PATCH, 1), 0)
    for b in range(ROWS // GROUP):
        part = slice(GROUP * b, GROUP * (b + 1))
        chosen = jnp.where(position[0:1, part] == index, 1.0, 0.0).astype(BF16)
        home = jnp.dot(returned_t[...], chosen, preferred_element_type=F32).T
        residual = enriched[part, :].astype(F32) + home
        normed = layer_norm(residual, gain[...], shift[...]).astype(BF16)
        inner = jnp.dot(normed, fc1[...], preferred_element_type=F32)
        hidden = (0.5 * inner * (1.0 + lax.erf(inner * (0.5 ** 0.5)))).astype(BF16)
        output[part, :] = (
            residual + jnp.dot(hidden, fc2[...], preferred_element_type=F32)
        ).astype(BF16)


PARAMS = pltpu.CompilerParams(vmem_limit_bytes=56 * 2**20)
WIRE = jax.ShapeDtypeStruct((128, 16, 128), BF16)


def encode(ext, brick, row, valid, dest, weight, linear, gain, shift):
    return pl.pallas_call(
        encode_kernel,
        out_shape=(
            jax.ShapeDtypeStruct((ROWS, C), BF16), WIRE, WIRE,
            jax.ShapeDtypeStruct((1, ROWS), jnp.int32),
        ),
        scratch_shapes=[
            pltpu.VMEM((C, 2048), BF16),
            pltpu.VMEM((C, KOFF * C), BF16),
            pltpu.VMEM((KOFF, ROWS), jnp.int32),
            pltpu.VMEM((KOFF * C, GROUP), BF16),
        ],
        compiler_params=PARAMS,
        name="encode",
    )(ext, brick, row, valid, dest, weight, linear, gain, shift)


def attend(arrived, gain, shift, qkv_weight, proj):
    return pl.pallas_call(
        attend_kernel,
        out_shape=WIRE,
        scratch_shapes=[
            pltpu.VMEM((PATCH, C), BF16),
            pltpu.VMEM((HEADS, 128, PATCH), BF16),
            pltpu.VMEM((HEADS, 2 * HEAD, PATCH), BF16),
            pltpu.VMEM((HEADS, HEAD, PATCH), BF16),
        ],
        compiler_params=PARAMS,
        cost_estimate=pl.CostEstimate(flops=20 * 10**9, bytes_accessed=2**21, transcendentals=2**24),
        name="attend",
    )(arrived, gain, shift, qkv_weight, proj)


def finish(returned0, returned1, enriched, position, gain, shift, fc1, fc2):
    return pl.pallas_call(
        finish_kernel,
        out_shape=jax.ShapeDtypeStruct((ROWS, C), BF16),
        scratch_shapes=[pltpu.VMEM((C, 2 * PATCH), BF16)],
        compiler_params=PARAMS,
        name="finish",
    )(returned0, returned1, enriched, position, gain, shift, fc1, fc2)


def exchange(block):
    return lax.all_to_all(block, "space", split_axis=0, concat_axis=0, tiled=True)


def padded(block, width):
    count = lax.axis_size("space")
    forward = [(i, i + 1) for i in range(count - 1)]
    backward = [(i + 1, i) for i in range(count - 1)]
    low = lax.ppermute(block[block.shape[0] - width :], "space", forward)
    high = lax.ppermute(block[:width], "space", backward)
    return jnp.concatenate([low, block, high], axis=0)


def per_device(
    feats, nbr_brick, nbr_row, nbr_valid, dest, conv_weight, cpe_linear, cpe_gain, cpe_shift,
    norm1_gain, norm1_shift, qkv_weight, proj_weight, norm2_gain, norm2_shift, fc1_weight,
    fc2_weight,
):
    line = lambda v: v.reshape(1, C)
    ext = padded(feats, HB * BR)
    enriched, out0, out1, position = encode(
        ext, nbr_brick, nbr_row, nbr_valid, dest.reshape(1, ROWS), conv_weight, cpe_linear,
        line(cpe_gain), line(cpe_shift),
    )
    back = []
    arrived = [exchange(out0), exchange(out1)]
    for block in arrived:
        back.append(exchange(
            attend(block, line(norm1_gain), line(norm1_shift), qkv_weight, proj_weight)
        ))
    return finish(
        back[0], back[1], enriched, position, line(norm2_gain), line(norm2_shift), fc1_weight,
        fc2_weight,
    )


def solution(mesh):
    placed = (
        P("space", None), P(None, "space"), P(None, "space"), P(None, "space"), P("space", None),
        P(), P(), P(), P(), P(), P(), P(), P(), P(), P(), P(), P(),
    )
    return jax.shard_map(
        per_device, mesh=mesh, in_specs=placed, out_specs=P("space", None), check_vma=False
    )
```

```python
import functools

import jax
import jax.numpy as jnp
from jax import lax
from jax.experimental import pallas as pl
from jax.experimental.pallas import tpu as pltpu
from jax.sharding import PartitionSpec as P

HEADS = 16
HEAD = 16
C = 256
PATCH = 1024
BR = 64
HB = 4
KOFF = 27
DEVICES = 128
ROWS = 1536
GROUP = 256
WINDOW = 768
LOG2E = 1.4426950408889634
SAFE_SCORE = 60.0
EMPTY = 1024.0
F32 = jnp.float32
BF16 = jnp.bfloat16


def layer_norm(values, gain, shift):
    average = jnp.mean(values, axis=-1, keepdims=True)
    centred = values - average
    spread = jnp.mean(centred * centred, axis=-1, keepdims=True)
    return centred * lax.rsqrt(spread + 1e-05) * gain + shift


def to_wire(rows):
    shaped = rows.reshape(128, 8, C)
    return jnp.concatenate([shaped[:, :, :128], shaped[:, :, 128:]], axis=1).astype(BF16)


def from_wire(block):
    wide = block.astype(F32)
    return jnp.concatenate([wide[:, :8], wide[:, 8:]], axis=2).reshape(PATCH, C)


def greet(barrier):
    me = lax.axis_index("space")

    def signal(step, carry):
        pl.semaphore_signal(
            barrier, inc=1, device_id=(lax.rem(me + step, DEVICES),),
            device_id_type=pl.DeviceIdType.MESH,
        )
        return carry

    lax.fori_loop(1, DEVICES, signal, 0)


def send_all(source, target, send_sem, recv_sem):
    me = lax.axis_index("space")

    def start(step, carry):
        other = lax.rem(me + step, DEVICES)
        pltpu.make_async_remote_copy(
            src_ref=source.at[other], dst_ref=target.at[me], send_sem=send_sem, recv_sem=recv_sem,
            device_id=(other,), device_id_type=pl.DeviceIdType.MESH,
        ).start()
        return carry

    lax.fori_loop(1, DEVICES, start, 0)
    pltpu.make_async_copy(source.at[me], target.at[me], recv_sem).start()


def wait_all(source, target, send_sem, recv_sem):
    sent = source.at[pl.ds(0, DEVICES - 1)]
    pltpu.make_async_copy(sent, sent, send_sem).wait()
    pltpu.make_async_copy(target, target, recv_sem).wait()


def encode_kernel(
    feats, brick, row, valid, dest, weight, linear, gain, shift,
    enriched, arrived0, arrived1, position,
    ext_t, weight_t, relative, picked, low, high, out0, out1, send_sem, recv_sem,
):
    me = lax.axis_index("space")
    barrier = pltpu.get_barrier_semaphore()
    greet(barrier)

    own_t = HB * BR // GROUP
    for i in range(ROWS // GROUP):
        ext_t[:, GROUP * (i + own_t) : GROUP * (i + own_t + 1)] = feats[GROUP * i : GROUP * (i + 1), :].T

    def turn_weight(k, carry):
        weight_t[:, pl.ds(pl.multiple_of(k * C, C), C)] = weight[k].T
        return carry

    lax.fori_loop(0, KOFF, turn_weight, 0)
    base = lax.broadcasted_iota(jnp.int32, (KOFF, ROWS), 1) // GROUP * GROUP
    reach = brick[...] * BR + row[...]
    lowest = jnp.where(me == 0, HB * BR, 0)
    highest = jnp.where(me == DEVICES - 1, ROWS + HB * BR, ROWS + 2 * HB * BR)
    counted = (valid[...] > 0) & (reach >= lowest) & (reach < highest)
    relative[...] = jnp.where(counted, reach - base, -1)
    place = lax.broadcasted_iota(jnp.int32, (WINDOW, 1), 0)

    def conv_group(g):
        columns = pl.ds(pl.multiple_of(g * GROUP, GROUP), GROUP)
        window = ext_t[:, pl.ds(pl.multiple_of(g * GROUP, GROUP), WINDOW)]
        for k in range(KOFF):
            chosen = jnp.where(relative[k : k + 1, columns] == place, 1.0, 0.0).astype(BF16)
            picked[C * k : C * (k + 1), :] = jnp.dot(
                window, chosen, preferred_element_type=F32
            ).astype(BF16)
        summed = jnp.dot(weight_t[...], picked[...], preferred_element_type=F32)
        convolved = summed.astype(BF16).T
        projected = jnp.dot(convolved, linear[...], preferred_element_type=F32)
        own = feats[columns, :].astype(F32)
        enriched[columns, :] = (own + layer_norm(projected, gain[...], shift[...])).astype(BF16)

    def inner_group(g, carry):
        conv_group(g)
        return carry

    lax.fori_loop(1, 3, inner_group, 0)
    pl.semaphore_wait(barrier, DEVICES - 1)
    width = HB * BR
    up = pltpu.make_async_remote_copy(
        src_ref=feats.at[pl.ds(ROWS - width, width)], dst_ref=low, send_sem=send_sem.at[2],
        recv_sem=recv_sem.at[2], device_id=(lax.rem(me + 1, DEVICES),),
        device_id_type=pl.DeviceIdType.MESH,
    )
    down = pltpu.make_async_remote_copy(
        src_ref=feats.at[pl.ds(0, width)], dst_ref=high, send_sem=send_sem.at[3],
        recv_sem=recv_sem.at[3], device_id=(lax.rem(me + DEVICES - 1, DEVICES),),
        device_id_type=pl.DeviceIdType.MESH,
    )
    up.start()
    down.start()
    lax.fori_loop(3, 5, inner_group, 0)
    up.wait()
    down.wait()
    ext_t[:, :GROUP] = low[...].T
    ext_t[:, ROWS + GROUP :] = high[...].T

    def outer_group(i, carry):
        conv_group(i * (ROWS // GROUP - 1))
        return carry

    lax.fori_loop(0, 2, outer_group, 0)

    owner = lax.broadcasted_iota(jnp.int32, (128, 1), 0)
    before = jnp.where(
        lax.broadcasted_iota(jnp.int32, (GROUP, GROUP), 0)
        < lax.broadcasted_iota(jnp.int32, (GROUP, GROUP), 1), 1.0, 0.0,
    ).astype(BF16)
    count = jnp.zeros((128, 1), F32)
    for b in range(ROWS // GROUP):
        part = slice(GROUP * b, GROUP * (b + 1))
        target = dest[0:1, part]
        named = jnp.where(target == owner, 1.0, 0.0)
        running = jnp.dot(named.astype(BF16), before, preferred_element_type=F32) + count
        slot = jnp.sum(running * named, axis=0, keepdims=True).astype(jnp.int32)
        count = count + jnp.sum(named, axis=1, keepdims=True)
        position[0:1, part] = jnp.where(slot < 8, 0, PATCH) + target * 8 + slot % 8

    counts = jnp.broadcast_to(count, (128, 128)).astype(BF16)
    expand = jnp.where(
        lax.broadcasted_iota(jnp.int32, (PATCH, 128), 0) // 8
        == lax.broadcasted_iota(jnp.int32, (PATCH, 128), 1), 1.0, 0.0,
    ).astype(BF16)
    filled = jnp.dot(expand, counts, preferred_element_type=F32)
    filled = jnp.concatenate([filled, filled], axis=1)
    slots = (lax.broadcasted_iota(jnp.int32, (PATCH, C), 0) % 8).astype(F32)
    where_to = position[...]
    for patch, out in enumerate((out0, out1)):
        index = lax.broadcasted_iota(jnp.int32, (PATCH, 1), 0) + patch * PATCH
        chosen = jnp.where(index == where_to, 1.0, 0.0).astype(BF16)
        moved = jnp.dot(chosen, enriched[...], preferred_element_type=F32)
        out[...] = to_wire(jnp.where(slots + 8.0 * patch < filled, moved, EMPTY))
        arrived = (arrived0, arrived1)[patch]
        send_all(out, arrived, send_sem.at[patch], recv_sem.at[patch])
    wait_all(out0, arrived0, send_sem.at[0], recv_sem.at[0])
    wait_all(out1, arrived1, send_sem.at[1], recv_sem.at[1])


def attend_kernel(
    arrived, gain, shift, qkv_weight, proj, attended,
    keys, query_t, value_t, mixed_t,
):
    rows = from_wire(arrived[...])
    occupied = rows[:, 0:1] < 0.5 * EMPTY
    rows = jnp.where(occupied, rows, 0.0)
    normed = layer_norm(rows, gain[...], shift[...]).astype(BF16)
    qkv = jnp.dot(normed, qkv_weight[...], preferred_element_type=F32).astype(BF16)
    queries = qkv[:, :C]
    keys[...] = qkv[:, C : 2 * C]
    values = jnp.where(occupied, qkv[:, 2 * C :], BF16(0))
    ones = jnp.broadcast_to(jnp.where(occupied, 1.0, 0.0), (PATCH, 128)).astype(BF16).T

    member = jnp.where(
        lax.broadcasted_iota(jnp.int32, (C, 128), 0) // HEAD
        == lax.broadcasted_iota(jnp.int32, (C, 128), 1), 1.0, 0.0,
    ).astype(BF16)

    def largest_square(table):
        wide = table.astype(F32)
        squares = jnp.dot((wide * wide).astype(BF16), member, preferred_element_type=F32)
        return jnp.max(squares, axis=0, keepdims=True)

    bound = jnp.max(largest_square(queries) * largest_square(qkv[:, C : 2 * C])) / HEAD
    safe = bound < SAFE_SCORE * SAFE_SCORE

    turned = (queries * BF16(HEAD ** (-0.5))).T
    values_t = values.T
    channel = lax.broadcasted_iota(jnp.int32, (128, 1), 0) // HEAD
    for h in range(HEADS):
        half, inside = h // 8, h % 8
        query_t[h] = jnp.where(channel == inside, turned[128 * half : 128 * (half + 1), :], BF16(0))
        value_t[h, :HEAD] = values_t[HEAD * h : HEAD * (h + 1), :]
        value_t[h, HEAD:] = ones[:HEAD, :]

    def finish(h, products, columns):
        below = products[HEAD : HEAD + 1, :]
        below = jnp.where(below > 0, below, 1.0)
        mixed_t[h, :, columns] = (products[:HEAD, :] / below).astype(BF16)

    block = 512

    @pl.when(safe)
    def _():
        def step(t, carry):
            half, column = t // (PATCH // block), t % (PATCH // block)
            columns = pl.ds(pl.multiple_of(column * block, block), block)
            some = keys[:, pl.ds(pl.multiple_of(half * 128, 128), 128)]
            for inside in range(8):
                h = half * 8 + inside
                scores = jnp.dot(some, query_t[h, :, columns], preferred_element_type=F32)
                weights = jnp.exp2(scores * LOG2E).astype(BF16)
                finish(h, jnp.dot(value_t[h], weights, preferred_element_type=F32), columns)
            return carry

        lax.fori_loop(0, 2 * (PATCH // block), step, 0)

    @pl.when(jnp.logical_not(safe))
    def _():
        penalty = jnp.where(occupied, 0.0, -1e30)

        def step(t, carry):
            h, column = t // (PATCH // 128), t % (PATCH // 128)
            columns = pl.ds(pl.multiple_of(column * 128, 128), 128)
            some = keys[:, pl.ds(pl.multiple_of(h // 8 * 128, 128), 128)]
            scores = jnp.dot(some, query_t[h, :, columns], preferred_element_type=F32)
            scores = jnp.where(penalty < 0.0, penalty, scores)
            highest = jnp.max(scores, axis=0, keepdims=True)
            weights = jnp.exp(scores - highest).astype(BF16)
            finish(h, jnp.dot(value_t[h], weights, preferred_element_type=F32), columns)
            return carry

        lax.fori_loop(0, HEADS * (PATCH // 128), step, 0)

    mixed = mixed_t[...].reshape(C, PATCH).T
    attended[...] = to_wire(jnp.dot(mixed, proj[...], preferred_element_type=F32))


def finish_kernel(
    attended0, attended1, enriched, position, gain, shift, fc1, fc2, output,
    returned0, returned1, returned_t, chosen, send_sem, recv_sem,
):
    barrier = pltpu.get_barrier_semaphore()
    greet(barrier)
    pl.semaphore_wait(barrier, DEVICES - 1)
    send_all(attended0, returned0, send_sem.at[0], recv_sem.at[0])
    send_all(attended1, returned1, send_sem.at[1], recv_sem.at[1])
    index = lax.broadcasted_iota(jnp.int32, (2 * PATCH, 1), 0)
    for b in range(ROWS // GROUP):
        part = slice(GROUP * b, GROUP * (b + 1))
        chosen[:, part] = jnp.where(position[0:1, part] == index, 1.0, 0.0).astype(BF16)
    wait_all(attended0, returned0, send_sem.at[0], recv_sem.at[0])
    wait_all(attended1, returned1, send_sem.at[1], recv_sem.at[1])
    for patch, block in enumerate((returned0, returned1)):
        returned_t[:, PATCH * patch : PATCH * (patch + 1)] = from_wire(block[...]).astype(BF16).T
    for b in range(ROWS // GROUP):
        part = slice(GROUP * b, GROUP * (b + 1))
        home = jnp.dot(returned_t[...], chosen[:, part], preferred_element_type=F32).T
        residual = enriched[part, :].astype(F32) + home
        normed = layer_norm(residual, gain[...], shift[...]).astype(BF16)
        inner = jnp.dot(normed, fc1[...], preferred_element_type=F32)
        hidden = (0.5 * inner * (1.0 + lax.erf(inner * (0.5 ** 0.5)))).astype(BF16)
        output[part, :] = (
            residual + jnp.dot(hidden, fc2[...], preferred_element_type=F32)
        ).astype(BF16)


def remote_params(number):
    return pltpu.CompilerParams(
        collective_id=number, has_side_effects=True, vmem_limit_bytes=56 * 2**20
    )


VMEM = pl.BlockSpec(memory_space=pltpu.VMEM)
PARAMS = pltpu.CompilerParams(vmem_limit_bytes=56 * 2**20)
WIRE = jax.ShapeDtypeStruct((128, 16, 128), BF16)


def encode(feats, brick, row, valid, dest, weight, linear, gain, shift):
    return pl.pallas_call(
        encode_kernel,
        out_shape=(
            jax.ShapeDtypeStruct((ROWS, C), BF16), WIRE, WIRE,
            jax.ShapeDtypeStruct((1, ROWS), jnp.int32),
        ),
        scratch_shapes=[
            pltpu.VMEM((C, 2048), BF16),
            pltpu.VMEM((C, KOFF * C), BF16),
            pltpu.VMEM((KOFF, ROWS), jnp.int32),
            pltpu.VMEM((KOFF * C, GROUP), BF16),
            pltpu.VMEM((HB * BR, C), BF16),
            pltpu.VMEM((HB * BR, C), BF16),
            pltpu.VMEM((128, 16, 128), BF16),
            pltpu.VMEM((128, 16, 128), BF16),
            pltpu.SemaphoreType.DMA((4,)),
            pltpu.SemaphoreType.DMA((4,)),
        ],
        in_specs=[VMEM] * 9,
        out_specs=[VMEM] * 4,
        compiler_params=remote_params(0),
        name="encode",
    )(feats, brick, row, valid, dest, weight, linear, gain, shift)


def attend(arrived, gain, shift, qkv_weight, proj):
    return pl.pallas_call(
        attend_kernel,
        out_shape=WIRE,
        scratch_shapes=[
            pltpu.VMEM((PATCH, C), BF16),
            pltpu.VMEM((HEADS, 128, PATCH), BF16),
            pltpu.VMEM((HEADS, 2 * HEAD, PATCH), BF16),
            pltpu.VMEM((HEADS, HEAD, PATCH), BF16),
        ],
        compiler_params=PARAMS,
        cost_estimate=pl.CostEstimate(flops=20 * 10**9, bytes_accessed=2**21, transcendentals=2**24),
        name="attend",
    )(arrived, gain, shift, qkv_weight, proj)


def finish(attended0, attended1, enriched, position, gain, shift, fc1, fc2):
    return pl.pallas_call(
        finish_kernel,
        out_shape=jax.ShapeDtypeStruct((ROWS, C), BF16),
        scratch_shapes=[
            pltpu.VMEM((128, 16, 128), BF16),
            pltpu.VMEM((128, 16, 128), BF16),
            pltpu.VMEM((C, 2 * PATCH), BF16),
            pltpu.VMEM((2 * PATCH, ROWS), BF16),
            pltpu.SemaphoreType.DMA((2,)),
            pltpu.SemaphoreType.DMA((2,)),
        ],
        in_specs=[VMEM] * 8,
        out_specs=VMEM,
        compiler_params=remote_params(1),
        name="finish",
    )(attended0, attended1, enriched, position, gain, shift, fc1, fc2)


def per_device(
    feats, nbr_brick, nbr_row, nbr_valid, dest, conv_weight, cpe_linear, cpe_gain, cpe_shift,
    norm1_gain, norm1_shift, qkv_weight, proj_weight, norm2_gain, norm2_shift, fc1_weight,
    fc2_weight,
):
    line = lambda v: v.reshape(1, C)
    enriched, arrived0, arrived1, position = encode(
        feats, nbr_brick, nbr_row, nbr_valid, dest.reshape(1, ROWS), conv_weight, cpe_linear,
        line(cpe_gain), line(cpe_shift),
    )
    attended0, attended1 = [
        attend(block, line(norm1_gain), line(norm1_shift), qkv_weight, proj_weight)
        for block in (arrived0, arrived1)
    ]
    return finish(
        attended0, attended1, enriched, position, line(norm2_gain), line(norm2_shift), fc1_weight,
        fc2_weight,
    )


def solution(mesh):
    placed = (
        P("space", None), P(None, "space"), P(None, "space"), P(None, "space"), P("space", None),
        P(), P(), P(), P(), P(), P(), P(), P(), P(), P(), P(), P(),
    )
    return jax.shard_map(
        per_device, mesh=mesh, in_specs=placed, out_specs=P("space", None), check_vma=False
    )
```

```python
import jax
import jax.numpy as jnp
from jax import lax
from jax.experimental import pallas as pl
from jax.experimental.pallas import tpu as pltpu
from jax.sharding import PartitionSpec as P

HEADS = 16
HEAD = 16
C = 256
PATCH = 1024
BR = 64
HB = 4
PATCH_DEV = 2
KOFF = 27
DEVICES = 128
ROWS = 1536
GROUP = 256
WINDOW = 768
LOG2E = 1.4426950408889634
SAFE_SCORE = 60.0
EMPTY = 1024.0
MARK = 1e38
F32 = jnp.float32
BF16 = jnp.bfloat16


def layer_norm(values, gain, shift):
    average = jnp.mean(values, axis=-1, keepdims=True)
    centred = values - average
    spread = jnp.mean(centred * centred, axis=-1, keepdims=True)
    return centred * lax.rsqrt(spread + 1e-05) * gain + shift


def to_wire(rows):
    shaped = rows.reshape(128, 8, C)
    return jnp.concatenate([shaped[:, :, :128], shaped[:, :, 128:]], axis=1).astype(BF16)


def from_wire(block):
    wide = block.astype(F32)
    return jnp.concatenate([wide[:, :8], wide[:, 8:]], axis=2).reshape(PATCH, C)


def greet(barrier):
    me = lax.axis_index("space")

    def signal(step, carry):
        pl.semaphore_signal(
            barrier, inc=1, device_id=(lax.rem(me + step, DEVICES),),
            device_id_type=pl.DeviceIdType.MESH,
        )
        return carry

    lax.fori_loop(1, DEVICES, signal, 0)


def send_all(source, target, send_sem, recv_sem):
    me = lax.axis_index("space")

    def start(step, carry):
        other = lax.rem(me + step, DEVICES)
        pltpu.make_async_remote_copy(
            src_ref=source.at[other], dst_ref=target.at[me], send_sem=send_sem, recv_sem=recv_sem,
            device_id=(other,), device_id_type=pl.DeviceIdType.MESH,
        ).start()
        return carry

    lax.fori_loop(1, DEVICES, start, 0)
    pltpu.make_async_copy(source.at[me], target.at[me], recv_sem).start()


def wait_all(source, target, send_sem, recv_sem):
    sent = source.at[pl.ds(0, DEVICES - 1)]
    pltpu.make_async_copy(sent, sent, send_sem).wait()
    pltpu.make_async_copy(target, target, recv_sem).wait()


def encode(
    feats, brick, row, valid, dest, weight, linear, gain, shift,
    enriched, outgoing, arrived, position,
    ext_t, weight_t, relative, picked, low, high, send_sem, recv_sem,
):
    me = lax.axis_index("space")
    barrier = pltpu.get_barrier_semaphore()
    greet(barrier)

    own_t = HB * BR // GROUP
    for i in range(ROWS // GROUP):
        ext_t[:, GROUP * (i + own_t) : GROUP * (i + own_t + 1)] = feats[GROUP * i : GROUP * (i + 1), :].T

    def turn_weight(k, carry):
        weight_t[:, pl.ds(pl.multiple_of(k * C, C), C)] = weight[k].T
        return carry

    lax.fori_loop(0, KOFF, turn_weight, 0)
    base = lax.broadcasted_iota(jnp.int32, (KOFF, ROWS), 1) // GROUP * GROUP
    reach = brick[...] * BR + row[...]
    lowest = jnp.where(me == 0, HB * BR, 0)
    highest = jnp.where(me == DEVICES - 1, ROWS + HB * BR, ROWS + 2 * HB * BR)
    counted = (valid[...] > 0) & (reach >= lowest) & (reach < highest)
    relative[...] = jnp.where(counted, reach - base, -1)
    place = lax.broadcasted_iota(jnp.int32, (WINDOW, 1), 0)

    def conv_group(g):
        columns = pl.ds(pl.multiple_of(g * GROUP, GROUP), GROUP)
        window = ext_t[:, pl.ds(pl.multiple_of(g * GROUP, GROUP), WINDOW)]
        for k in range(KOFF):
            chosen = jnp.where(relative[k : k + 1, columns] == place, 1.0, 0.0).astype(BF16)
            picked[C * k : C * (k + 1), :] = jnp.dot(
                window, chosen, preferred_element_type=F32
            ).astype(BF16)
        summed = jnp.dot(weight_t[...], picked[...], preferred_element_type=F32)
        convolved = summed.astype(BF16).T
        projected = jnp.dot(convolved, linear[...], preferred_element_type=F32)
        own = feats[columns, :].astype(F32)
        enriched[columns, :] = (own + layer_norm(projected, gain[...], shift[...])).astype(BF16)

    def inner_group(g, carry):
        conv_group(g)
        return carry

    lax.fori_loop(1, 3, inner_group, 0)
    pl.semaphore_wait(barrier, DEVICES - 1)
    width = HB * BR
    up = pltpu.make_async_remote_copy(
        src_ref=feats.at[pl.ds(ROWS - width, width)], dst_ref=low, send_sem=send_sem.at[4],
        recv_sem=recv_sem.at[4], device_id=(lax.rem(me + 1, DEVICES),),
        device_id_type=pl.DeviceIdType.MESH,
    )
    down = pltpu.make_async_remote_copy(
        src_ref=feats.at[pl.ds(0, width)], dst_ref=high, send_sem=send_sem.at[5],
        recv_sem=recv_sem.at[5], device_id=(lax.rem(me + DEVICES - 1, DEVICES),),
        device_id_type=pl.DeviceIdType.MESH,
    )
    up.start()
    down.start()
    lax.fori_loop(3, 5, inner_group, 0)
    up.wait()
    down.wait()
    ext_t[:, :GROUP] = low[...].T
    ext_t[:, ROWS + GROUP :] = high[...].T

    def outer_group(i, carry):
        conv_group(i * (ROWS // GROUP - 1))
        return carry

    lax.fori_loop(0, 2, outer_group, 0)

    owner = lax.broadcasted_iota(jnp.int32, (128, 1), 0)
    before = jnp.where(
        lax.broadcasted_iota(jnp.int32, (GROUP, GROUP), 0)
        < lax.broadcasted_iota(jnp.int32, (GROUP, GROUP), 1), 1.0, 0.0,
    ).astype(BF16)
    count = jnp.zeros((128, 1), F32)
    for b in range(ROWS // GROUP):
        part = slice(GROUP * b, GROUP * (b + 1))
        target = dest[0:1, part]
        named = jnp.where(target == owner, 1.0, 0.0)
        running = jnp.dot(named.astype(BF16), before, preferred_element_type=F32) + count
        slot = jnp.sum(running * named, axis=0, keepdims=True).astype(jnp.int32)
        count = count + jnp.sum(named, axis=1, keepdims=True)
        position[0:1, part] = jnp.where(slot < 8, 0, PATCH) + target * 8 + slot % 8

    counts = jnp.broadcast_to(count, (128, 128)).astype(BF16)
    expand = jnp.where(
        lax.broadcasted_iota(jnp.int32, (PATCH, 128), 0) // 8
        == lax.broadcasted_iota(jnp.int32, (PATCH, 128), 1), 1.0, 0.0,
    ).astype(BF16)
    filled = jnp.dot(expand, counts, preferred_element_type=F32)
    filled = jnp.concatenate([filled, filled], axis=1)
    slots = (lax.broadcasted_iota(jnp.int32, (PATCH, C), 0) % 8).astype(F32)
    where_to = position[...]
    for patch in range(2):
        index = lax.broadcasted_iota(jnp.int32, (PATCH, 1), 0) + patch * PATCH
        chosen = jnp.where(index == where_to, 1.0, 0.0).astype(BF16)
        moved = jnp.dot(chosen, enriched[...], preferred_element_type=F32)
        outgoing[patch] = to_wire(jnp.where(slots + 8.0 * patch < filled, moved, EMPTY))
        send_all(outgoing.at[patch], arrived.at[patch], send_sem.at[patch], recv_sem.at[patch])


def attend(
    arrived, gain, shift, qkv_weight, proj, attended, keys, query_t, value_t, mixed_t
):
    rows = from_wire(arrived[...])
    occupied = rows[:, 0:1] < 0.5 * EMPTY
    rows = jnp.where(occupied, rows, 0.0)
    normed = layer_norm(rows, gain[...], shift[...]).astype(BF16)
    qkv = jnp.dot(normed, qkv_weight[...], preferred_element_type=F32).astype(BF16)
    queries = qkv[:, :C]
    keys[...] = qkv[:, C : 2 * C]
    values = jnp.where(occupied, qkv[:, 2 * C :], BF16(0))
    ones = jnp.broadcast_to(jnp.where(occupied, 1.0, 0.0), (PATCH, 128)).astype(BF16).T

    member = jnp.where(
        lax.broadcasted_iota(jnp.int32, (C, 128), 0) // HEAD
        == lax.broadcasted_iota(jnp.int32, (C, 128), 1), 1.0, 0.0,
    ).astype(BF16)

    def largest_square(table):
        wide = table.astype(F32)
        squares = jnp.dot((wide * wide).astype(BF16), member, preferred_element_type=F32)
        return jnp.max(squares, axis=0, keepdims=True)

    bound = jnp.max(
        largest_square(queries) * largest_square(qkv[:, C : 2 * C]), axis=1, keepdims=True
    ) / HEAD
    safe = bound < SAFE_SCORE * SAFE_SCORE

    turned = (queries * BF16(HEAD ** (-0.5))).T
    values_t = values.T
    channel = lax.broadcasted_iota(jnp.int32, (128, 1), 0) // HEAD
    for h in range(HEADS):
        half, inside = h // 8, h % 8
        query_t[h] = jnp.where(channel == inside, turned[128 * half : 128 * (half + 1), :], BF16(0))
        value_t[h, :HEAD] = values_t[HEAD * h : HEAD * (h + 1), :]
        value_t[h, HEAD:] = ones[:HEAD, :]

    def finish_head(h, products, columns):
        below = products[HEAD : HEAD + 1, :]
        below = jnp.where(below > 0, below, 1.0)
        mixed_t[h, :, columns] = (products[:HEAD, :] / below).astype(BF16)

    block = 512

    def step(t, carry):
        half, column = t // (PATCH // block), t % (PATCH // block)
        columns = pl.ds(pl.multiple_of(column * block, block), block)
        some = keys[:, pl.ds(pl.multiple_of(half * 128, 128), 128)]
        for inside in range(8):
            h = half * 8 + inside
            scores = jnp.dot(some, query_t[h, :, columns], preferred_element_type=F32)
            weights = jnp.exp2(scores * LOG2E).astype(BF16)
            finish_head(h, jnp.dot(value_t[h], weights, preferred_element_type=F32), columns)
        return carry

    lax.fori_loop(0, 2 * (PATCH // block), step, 0)
    mixed = mixed_t[...].reshape(C, PATCH).T
    result = jnp.dot(mixed, proj[...], preferred_element_type=F32)
    attended[...] = to_wire(jnp.where(jnp.broadcast_to(safe, (PATCH, 1)), result, MARK))


def transform(rows, attended, gain, shift, fc1, fc2, block_t):
    for b in range(PATCH // GROUP):
        part = slice(GROUP * b, GROUP * (b + 1))
        residual = rows[part] + attended[part]
        normed = layer_norm(residual, gain[...], shift[...]).astype(BF16)
        inner = jnp.dot(normed, fc1[...], preferred_element_type=F32)
        hidden = (0.5 * inner * (1.0 + lax.erf(inner * (0.5 ** 0.5)))).astype(BF16)
        finished = residual + jnp.dot(hidden, fc2[...], preferred_element_type=F32)
        block_t[:, part] = finished.astype(BF16).T


def block_kernel(
    feats, brick, row, valid, dest, weight, linear, cpe_gain, cpe_shift, norm1_gain, norm1_shift,
    qkv_weight, proj, norm2_gain, norm2_shift, fc1, fc2,
    output, marked,
    enriched, outgoing, arrived, attended, returned, position,
    ext_t, weight_t, relative, picked, low, high,
    keys, query_t, value_t, mixed_t, block_t, home_t, chosen, send_sem, recv_sem,
):
    encode(
        feats, brick, row, valid, dest, weight, linear, cpe_gain, cpe_shift,
        enriched, outgoing, arrived, position,
        ext_t, weight_t, relative, picked, low, high, send_sem, recv_sem,
    )

    def own_patch(patch, carry):
        wait_all(outgoing.at[patch], arrived.at[patch], send_sem.at[patch], recv_sem.at[patch])
        attend(
            arrived.at[patch], norm1_gain, norm1_shift, qkv_weight, proj, attended.at[patch],
            keys, query_t, value_t, mixed_t,
        )
        send_all(
            attended.at[patch], returned.at[patch], send_sem.at[2 + patch], recv_sem.at[2 + patch]
        )
        return carry

    lax.fori_loop(0, 2, own_patch, 0)

    index = lax.broadcasted_iota(jnp.int32, (2 * PATCH, 1), 0)
    for b in range(ROWS // GROUP):
        part = slice(GROUP * b, GROUP * (b + 1))
        chosen[:, part] = jnp.where(position[0:1, part] == index, 1.0, 0.0).astype(BF16)
    largest = jnp.zeros((1, C), F32)
    for patch in range(2):
        rows = from_wire(outgoing[patch])
        rows = jnp.where(rows[:, 0:1] < 0.5 * EMPTY, rows, 0.0)
        wait_all(
            attended.at[patch], returned.at[patch], send_sem.at[2 + patch], recv_sem.at[2 + patch]
        )
        back = from_wire(returned[patch])
        largest = jnp.maximum(largest, jnp.max(back, axis=0, keepdims=True))
        transform(rows, back, norm2_gain, norm2_shift, fc1, fc2, block_t)
        for b in range(ROWS // GROUP):
            part = slice(GROUP * b, GROUP * (b + 1))
            home = jnp.dot(
                block_t[...], chosen[PATCH * patch : PATCH * (patch + 1), part],
                preferred_element_type=F32,
            )
            if patch == 0:
                home_t[:, part] = home
            else:
                output[part, :] = (home_t[:, part] + home).astype(BF16).T
    marked[...] = jnp.broadcast_to(largest, (8, C))


VMEM = pl.BlockSpec(memory_space=pltpu.VMEM)
WIRE = (2, DEVICES, 16, 128)


def fused(*operands):
    return pl.pallas_call(
        block_kernel,
        out_shape=(
            jax.ShapeDtypeStruct((ROWS, C), BF16),
            jax.ShapeDtypeStruct((8, C), F32),
        ),
        in_specs=[VMEM] * 17,
        out_specs=(VMEM, VMEM),
        scratch_shapes=[
            pltpu.VMEM((ROWS, C), BF16),
            pltpu.VMEM(WIRE, BF16),
            pltpu.VMEM(WIRE, BF16),
            pltpu.VMEM(WIRE, BF16),
            pltpu.VMEM(WIRE, BF16),
            pltpu.VMEM((1, ROWS), jnp.int32),
            pltpu.VMEM((C, 2048), BF16),
            pltpu.VMEM((C, KOFF * C), BF16),
            pltpu.VMEM((KOFF, ROWS), jnp.int32),
            pltpu.VMEM((KOFF * C, GROUP), BF16),
            pltpu.VMEM((HB * BR, C), BF16),
            pltpu.VMEM((HB * BR, C), BF16),
            pltpu.VMEM((PATCH, C), BF16),
            pltpu.VMEM((HEADS, 128, PATCH), BF16),
            pltpu.VMEM((HEADS, 2 * HEAD, PATCH), BF16),
            pltpu.VMEM((HEADS, HEAD, PATCH), BF16),
            pltpu.VMEM((C, PATCH), BF16),
            pltpu.VMEM((C, ROWS), F32),
            pltpu.VMEM((2 * PATCH, ROWS), BF16),
            pltpu.SemaphoreType.DMA((6,)),
            pltpu.SemaphoreType.DMA((6,)),
        ],
        compiler_params=pltpu.CompilerParams(
            collective_id=0, has_side_effects=True, vmem_limit_bytes=58 * 2**20
        ),
        name="block",
    )(*operands)


def padded(block, sides, width):
    for axis, dim in sides:
        count = lax.axis_size(axis)
        forward = [(i, i + 1) for i in range(count - 1)]
        backward = [(target, source) for source, target in forward]
        low = lax.ppermute(
            lax.slice_in_dim(block, block.shape[dim] - width, None, axis=dim), axis, forward
        )
        high = lax.ppermute(lax.slice_in_dim(block, 0, width, axis=dim), axis, backward)
        block = jnp.concatenate([low, block, high], axis=dim)
    return block


def plain_attend(queries, keys, values, occupied):
    slot_count = queries.shape[0]
    patches = slot_count // PATCH
    groups = HEADS // 4

    def arrange(table):
        shaped = table.reshape(patches, PATCH, groups, 4, HEAD).transpose(0, 2, 1, 3, 4)
        return shaped.reshape(patches * groups, PATCH, 4, HEAD)

    masks = jnp.repeat(occupied.reshape(patches, PATCH), groups, axis=0)

    def one_group(items):
        query_part, key_part, value_part, mask_part = items
        scores = jnp.einsum(
            "qhd,khd->hqk", query_part, key_part, preferred_element_type=jnp.float32
        ) * HEAD ** (-0.5)
        scores = jnp.where(mask_part[None, None, :] > 0, scores, -1e30)
        highest = jnp.max(scores, axis=-1, keepdims=True)
        weights = jnp.exp(scores - highest)
        probable = (weights / jnp.sum(weights, axis=-1, keepdims=True)).astype(BF16)
        mixed = jnp.einsum("hqk,khd->qhd", probable, value_part, preferred_element_type=jnp.float32)
        return mixed.astype(BF16)

    mixed = lax.map(one_group, (arrange(queries), arrange(keys), arrange(values), masks))
    mixed = mixed.reshape(patches, groups, PATCH, 4, HEAD).transpose(0, 2, 1, 3, 4)
    return mixed.reshape(slot_count, HEADS * HEAD)


def plain_finish(base_rows, attended, norm2_gain, norm2_shift, fc1_weight, fc2_weight):
    residual = base_rows.astype(jnp.float32) + attended.astype(jnp.float32)
    normed_two = layer_norm(residual, norm2_gain, norm2_shift).astype(BF16)
    hidden = jax.nn.gelu(
        jnp.dot(normed_two, fc1_weight, preferred_element_type=jnp.float32), approximate=False
    ).astype(BF16)
    return (residual + jnp.dot(hidden, fc2_weight, preferred_element_type=jnp.float32)).astype(
        BF16
    )


def plain_block(
    feats,
    nbr_brick,
    nbr_row,
    nbr_valid,
    dest,
    conv_weight,
    cpe_linear,
    cpe_gain,
    cpe_shift,
    norm1_gain,
    norm1_shift,
    qkv_weight,
    proj_weight,
    norm2_gain,
    norm2_shift,
    fc1_weight,
    fc2_weight,
):
    channels = feats.shape[1]
    extended = padded(feats, (("space", 0),), HB * BR)
    neighbour = nbr_brick * BR + nbr_row
    picked = jnp.take(extended, neighbour, axis=0)
    picked = jnp.where(nbr_valid[:, :, None] > 0, picked, jnp.zeros((), BF16))
    convolved = jnp.einsum(
        "krc,kcd->rd", picked, conv_weight, preferred_element_type=jnp.float32
    ).astype(BF16)
    projected = jnp.dot(convolved, cpe_linear, preferred_element_type=jnp.float32)
    enriched = (feats.astype(jnp.float32) + layer_norm(projected, cpe_gain, cpe_shift)).astype(
        BF16
    )
    devices = lax.axis_size("space")
    slot_count = PATCH_DEV * PATCH
    capacity = slot_count // devices
    target = dest[:, 0]
    onehot = (target[:, None] == jnp.arange(devices, dtype=jnp.int32)[None, :]).astype(jnp.int32)
    running = jnp.cumsum(onehot, axis=0)
    within = jnp.sum((running - 1) * onehot, axis=1)
    position = target * capacity + within
    outgoing = jnp.zeros((devices * capacity, channels), BF16).at[position].set(enriched)
    flags_out = jnp.zeros((devices * capacity,), jnp.int32).at[position].set(1)
    arrived, flags_in = (
        lax.all_to_all(outgoing, "space", split_axis=0, concat_axis=0, tiled=True),
        lax.all_to_all(flags_out, "space", split_axis=0, concat_axis=0, tiled=True),
    )
    placed = (
        arrived.reshape(devices, capacity, channels)
        .transpose(1, 0, 2)
        .reshape(slot_count, channels)
    )
    occupied = flags_in.reshape(devices, capacity).transpose(1, 0).reshape(slot_count)
    normed = layer_norm(placed.astype(jnp.float32), norm1_gain, norm1_shift).astype(BF16)
    qkv = jnp.dot(normed, qkv_weight, preferred_element_type=jnp.float32).astype(BF16)
    mixed = plain_attend(
        qkv[:, :channels], qkv[:, channels : 2 * channels], qkv[:, 2 * channels :], occupied
    )
    attended = jnp.dot(mixed, proj_weight, preferred_element_type=jnp.float32).astype(BF16)
    finished = plain_finish(placed, attended, norm2_gain, norm2_shift, fc1_weight, fc2_weight)
    returned = lax.all_to_all(
        finished.reshape(capacity, devices, channels)
        .transpose(1, 0, 2)
        .reshape(slot_count, channels),
        "space",
        split_axis=0,
        concat_axis=0,
        tiled=True,
    )
    return jnp.take(returned, position, axis=0)


def per_device(
    feats, nbr_brick, nbr_row, nbr_valid, dest, conv_weight, cpe_linear, cpe_gain, cpe_shift,
    norm1_gain, norm1_shift, qkv_weight, proj_weight, norm2_gain, norm2_shift, fc1_weight,
    fc2_weight,
):
    line = lambda v: v.reshape(1, C)
    output, marked = fused(
        feats, nbr_brick, nbr_row, nbr_valid, dest.reshape(1, ROWS), conv_weight, cpe_linear,
        line(cpe_gain), line(cpe_shift), line(norm1_gain), line(norm1_shift), qkv_weight,
        proj_weight, line(norm2_gain), line(norm2_shift), fc1_weight, fc2_weight,
    )
    return lax.cond(
        marked[0, 0] < 0.1 * MARK,
        lambda: output,
        lambda: plain_block(
            feats, nbr_brick, nbr_row, nbr_valid, dest, conv_weight, cpe_linear, cpe_gain,
            cpe_shift, norm1_gain, norm1_shift, qkv_weight, proj_weight, norm2_gain, norm2_shift,
            fc1_weight, fc2_weight,
        ),
    )


def solution(mesh):
    placed = (
        P("space", None), P(None, "space"), P(None, "space"), P(None, "space"), P("space", None),
        P(), P(), P(), P(), P(), P(), P(), P(), P(), P(), P(), P(),
    )
    return jax.shard_map(
        per_device, mesh=mesh, in_specs=placed, out_specs=P("space", None), check_vma=False
    )
```

```python
import functools

import jax
import jax.numpy as jnp
from jax import lax
from jax.experimental import pallas as pl
from jax.experimental.pallas import tpu as pltpu
from jax.sharding import PartitionSpec as P

HEADS = 16
HEAD = 16
C = 256
PATCH = 1024
BR = 64
HB = 4
BLOCK = 512
KOFF = 27
DEVICES = 128
ROWS = 1536
GROUP = 256
WINDOW = 768
LOG2E = 1.4426950408889634
SAFE_SCORE = 60.0
EMPTY = 1024.0
MARK = 1e38
F32 = jnp.float32
BF16 = jnp.bfloat16


def layer_norm(values, gain, shift):
    average = jnp.mean(values, axis=-1, keepdims=True)
    centred = values - average
    spread = jnp.mean(centred * centred, axis=-1, keepdims=True)
    return centred * lax.rsqrt(spread + 1e-05) * gain + shift


def to_wire(rows):
    shaped = rows.reshape(rows.shape[0] // 8, 8, C)
    return jnp.concatenate([shaped[:, :, :128], shaped[:, :, 128:]], axis=1).astype(BF16)


def from_wire(block):
    wide = block.astype(F32)
    return jnp.concatenate([wide[:, :8], wide[:, 8:]], axis=2).reshape(PATCH, C)


def greet(barrier):
    me = lax.axis_index("space")

    def signal(step, carry):
        pl.semaphore_signal(
            barrier, inc=1, device_id=(lax.rem(me + step, DEVICES),),
            device_id_type=pl.DeviceIdType.MESH,
        )
        return carry

    lax.fori_loop(1, DEVICES, signal, 0)


def send_some(source, target, first, count, least, send_sem, recv_sem):
    me = lax.axis_index("space")

    def start(step, carry):
        other = first + lax.rem(me + step, count)
        pltpu.make_async_remote_copy(
            src_ref=source.at[other], dst_ref=target.at[me], send_sem=send_sem, recv_sem=recv_sem,
            device_id=(other,), device_id_type=pl.DeviceIdType.MESH,
        ).start()
        return carry

    lax.fori_loop(least, count, start, 0)


def keep_own(source, target, recv_sem):
    me = lax.axis_index("space")
    pltpu.make_async_copy(source.at[me], target.at[me], recv_sem).start()


def wait_all(source, target, send_sem, recv_sem):
    sent = source.at[pl.ds(0, DEVICES - 1)]
    pltpu.make_async_copy(sent, sent, send_sem).wait()
    pltpu.make_async_copy(target, target, recv_sem).wait()


def encode(
    feats, brick, row, valid, dest, weight, linear, gain, shift,
    enriched, outgoing, arrived, position,
    ext_t, weight_v, weight_t, relative, picked, low, high, send_sem, recv_sem, load_sem,
):
    me = lax.axis_index("space")
    barrier = pltpu.get_barrier_semaphore()
    loading = pltpu.make_async_copy(weight, weight_v, load_sem.at[0])
    loading.start()
    greet(barrier)

    own_t = HB * BR // GROUP
    for i in range(ROWS // GROUP):
        ext_t[:, GROUP * (i + own_t) : GROUP * (i + own_t + 1)] = feats[GROUP * i : GROUP * (i + 1), :].T

    base = lax.broadcasted_iota(jnp.int32, (KOFF, ROWS), 1) // GROUP * GROUP
    reach = brick[...] * BR + row[...]
    lowest = jnp.where(me == 0, HB * BR, 0)
    highest = jnp.where(me == DEVICES - 1, ROWS + HB * BR, ROWS + 2 * HB * BR)
    counted = (valid[...] > 0) & (reach >= lowest) & (reach < highest)
    relative[...] = jnp.where(counted, reach - base, -1)
    place = lax.broadcasted_iota(jnp.int32, (WINDOW, 1), 0)

    def conv_group(g, turn):
        columns = pl.ds(pl.multiple_of(g * GROUP, GROUP), GROUP)
        window = ext_t[:, pl.ds(pl.multiple_of(g * GROUP, GROUP), WINDOW)]
        for k in range(KOFF):
            if turn:
                weight_t[:, C * k : C * (k + 1)] = weight_v[k].T
            chosen = jnp.where(relative[k : k + 1, columns] == place, 1.0, 0.0).astype(BF16)
            picked[C * k : C * (k + 1), :] = jnp.dot(
                window, chosen, preferred_element_type=F32
            ).astype(BF16)
        summed = jnp.dot(weight_t[...], picked[...], preferred_element_type=F32)
        convolved = summed.astype(BF16).T
        projected = jnp.dot(convolved, linear[...], preferred_element_type=F32)
        own = feats[columns, :].astype(F32)
        enriched[columns, :] = (own + layer_norm(projected, gain[...], shift[...])).astype(BF16)

    width = HB * BR
    up = pltpu.make_async_remote_copy(
        src_ref=feats.at[pl.ds(ROWS - width, width)], dst_ref=low, send_sem=send_sem.at[4],
        recv_sem=recv_sem.at[4], device_id=(lax.rem(me + 1, DEVICES),),
        device_id_type=pl.DeviceIdType.MESH,
    )
    down = pltpu.make_async_remote_copy(
        src_ref=feats.at[pl.ds(0, width)], dst_ref=high, send_sem=send_sem.at[5],
        recv_sem=recv_sem.at[5], device_id=(lax.rem(me + DEVICES - 1, DEVICES),),
        device_id_type=pl.DeviceIdType.MESH,
    )
    loading.wait()
    conv_group(1, True)
    pl.semaphore_wait(barrier, DEVICES - 1)
    up.start()
    down.start()

    def later_group(i, carry):
        @pl.when(i == 4)
        def _():
            up.wait()
            down.wait()
            ext_t[:, :GROUP] = low[...].T
            ext_t[:, ROWS + GROUP :] = high[...].T

        conv_group(jnp.where(i < 4, i + 1, (i - 4) * 5), False)
        return carry

    lax.fori_loop(1, ROWS // GROUP, later_group, 0)

    owner = lax.broadcasted_iota(jnp.int32, (128, 1), 0)
    before = jnp.where(
        lax.broadcasted_iota(jnp.int32, (GROUP, GROUP), 0)
        < lax.broadcasted_iota(jnp.int32, (GROUP, GROUP), 1), 1.0, 0.0,
    ).astype(BF16)
    count = jnp.zeros((128, 1), F32)
    for b in range(ROWS // GROUP):
        part = slice(GROUP * b, GROUP * (b + 1))
        target = dest[0:1, part]
        named = jnp.where(target == owner, 1.0, 0.0)
        running = jnp.dot(named.astype(BF16), before, preferred_element_type=F32) + count
        slot = jnp.sum(running * named, axis=0, keepdims=True).astype(jnp.int32)
        count = count + jnp.sum(named, axis=1, keepdims=True)
        position[0:1, part] = jnp.where(slot < 8, 0, PATCH) + target * 8 + slot % 8

    counts = jnp.broadcast_to(count, (128, 128)).astype(BF16)
    expand = jnp.where(
        lax.broadcasted_iota(jnp.int32, (PATCH, 128), 0) // 8
        == lax.broadcasted_iota(jnp.int32, (PATCH, 128), 1), 1.0, 0.0,
    ).astype(BF16)
    filled = jnp.dot(expand, counts, preferred_element_type=F32)
    filled = jnp.concatenate([filled, filled], axis=1)
    slots = (lax.broadcasted_iota(jnp.int32, (PATCH, C), 0) % 8).astype(F32)
    where_to = position[...]
    for patch in range(2):
        index = lax.broadcasted_iota(jnp.int32, (PATCH, 1), 0) + patch * PATCH
        chosen = jnp.where(index == where_to, 1.0, 0.0).astype(BF16)
        moved = jnp.dot(chosen, enriched[...], preferred_element_type=F32)
        outgoing[patch] = to_wire(jnp.where(slots + 8.0 * patch < filled, moved, EMPTY))
        send_some(
            outgoing.at[patch], arrived.at[patch], 0, DEVICES, 1, send_sem.at[patch],
            recv_sem.at[patch],
        )
        keep_own(outgoing.at[patch], arrived.at[patch], recv_sem.at[patch])


def attend(
    exact, arrived, gain, shift, qkv_weight, proj, attended, returned, keys, query_t, value_t,
    mixed_t, send_sem, recv_sem,
):
    rows = from_wire(arrived[...])
    occupied = rows[:, 0:1] < 0.5 * EMPTY
    rows = jnp.where(occupied, rows, 0.0)
    normed = layer_norm(rows, gain[...], shift[...]).astype(BF16)
    qkv = jnp.dot(normed, qkv_weight[...], preferred_element_type=F32).astype(BF16)
    queries = qkv[:, :C]
    keys[...] = qkv[:, C : 2 * C]
    values = jnp.where(occupied, qkv[:, 2 * C :], BF16(0))
    ones = jnp.broadcast_to(jnp.where(occupied, 1.0, 0.0), (PATCH, 128)).astype(BF16).T

    member = jnp.where(
        lax.broadcasted_iota(jnp.int32, (C, 128), 0) // HEAD
        == lax.broadcasted_iota(jnp.int32, (C, 128), 1), 1.0, 0.0,
    ).astype(BF16)

    def largest_square(table):
        wide = table.astype(F32)
        squares = jnp.dot((wide * wide).astype(BF16), member, preferred_element_type=F32)
        return jnp.max(squares, axis=0, keepdims=True)

    bound = jnp.max(
        largest_square(queries) * largest_square(qkv[:, C : 2 * C]), axis=1, keepdims=True
    ) / HEAD
    safe = bound < SAFE_SCORE * SAFE_SCORE

    turned = (queries * BF16(HEAD ** (-0.5))).T
    values_t = values.T
    channel = lax.broadcasted_iota(jnp.int32, (128, 1), 0) // HEAD
    for h in range(HEADS):
        half, inside = h // 8, h % 8
        query_t[h] = jnp.where(channel == inside, turned[128 * half : 128 * (half + 1), :], BF16(0))
        value_t[h, :HEAD] = values_t[HEAD * h : HEAD * (h + 1), :]
        value_t[h, HEAD:] = ones[:HEAD, :]

    penalty = jnp.where(occupied, 0.0, -1e30)

    def head(h, some, columns):
        scores = jnp.dot(some, query_t[h, :, columns], preferred_element_type=F32)
        if exact:
            scores = jnp.where(penalty < 0.0, penalty, scores)
            scores = scores - jnp.max(scores, axis=0, keepdims=True)
        weights = jnp.exp2(scores * LOG2E).astype(BF16)
        products = jnp.dot(value_t[h], weights, preferred_element_type=F32)
        below = products[HEAD : HEAD + 1, :]
        below = jnp.where(below > 0, below, 1.0)
        return (products[:HEAD, :] / below).astype(BF16)

    me = lax.axis_index("space")
    near = BLOCK // 8

    def some_queries(turn, carry):
        block = lax.rem(me // near + turn, PATCH // BLOCK)
        start = pl.multiple_of(block * BLOCK, BLOCK)

        if exact:
            def one_head(t, carry):
                h, offset = t // (BLOCK // 128), t % (BLOCK // 128) * 128
                some = keys[:, pl.ds(pl.multiple_of(h // 8 * 128, 128), 128)]
                mixed_t[h, :, pl.ds(pl.multiple_of(offset, 128), 128)] = head(
                    h, some, pl.ds(pl.multiple_of(start + offset, 128), 128)
                )
                return carry

            lax.fori_loop(0, HEADS * (BLOCK // 128), one_head, 0)
        else:
            def eight_heads(half, carry):
                some = keys[:, pl.ds(pl.multiple_of(half * 128, 128), 128)]
                for inside in range(8):
                    h = half * 8 + inside
                    mixed_t[h] = head(h, some, pl.ds(start, BLOCK))
                return carry

            lax.fori_loop(0, HEADS // 8, eight_heads, 0)

        mixed = mixed_t[...].reshape(C, BLOCK).T
        result = jnp.dot(mixed, proj[...], preferred_element_type=F32)
        if not exact:
            result = jnp.where(jnp.broadcast_to(safe, (BLOCK, 1)), result, MARK)
        first = pl.multiple_of(block * near, near)
        attended[pl.ds(first, near)] = to_wire(result)

        @pl.when(turn == 0)
        def _():
            keep_own(attended, returned, recv_sem)

        send_some(
            attended, returned, first, near, jnp.where(turn == 0, 1, 0), send_sem, recv_sem
        )
        return carry

    lax.fori_loop(0, PATCH // BLOCK, some_queries, 0)


def transform(rows, attended, gain, shift, fc1, fc2, block_t):
    for b in range(PATCH // GROUP):
        part = slice(GROUP * b, GROUP * (b + 1))
        residual = rows[part] + attended[part]
        normed = layer_norm(residual, gain[...], shift[...]).astype(BF16)
        inner = jnp.dot(normed, fc1[...], preferred_element_type=F32)
        hidden = (0.5 * inner * (1.0 + lax.erf(inner * (0.5 ** 0.5)))).astype(BF16)
        finished = residual + jnp.dot(hidden, fc2[...], preferred_element_type=F32)
        block_t[:, part] = finished.astype(BF16).T


def block_kernel(
    exact,
    feats, brick, row, valid, dest, weight, linear, cpe_gain, cpe_shift, norm1_gain, norm1_shift,
    qkv_far, proj_far, norm2_gain, norm2_shift, fc1_far, fc2_far,
    output, marked,
    enriched, outgoing, arrived, attended, returned, position,
    ext_t, weight_v, weight_t, relative, picked, low, high, qkv_weight, proj, fc1, fc2,
    keys, query_t, value_t, mixed_t, block_t, home_t, chosen, send_sem, recv_sem, load_sem,
):
    loads = [
        pltpu.make_async_copy(far, near, load_sem.at[1 + i])
        for i, (far, near) in enumerate(
            ((qkv_far, qkv_weight), (proj_far, proj), (fc1_far, fc1), (fc2_far, fc2))
        )
    ]
    for load in loads:
        load.start()
    encode(
        feats, brick, row, valid, dest, weight, linear, cpe_gain, cpe_shift,
        enriched, outgoing, arrived, position,
        ext_t, weight_v, weight_t, relative, picked, low, high, send_sem, recv_sem, load_sem,
    )
    index = lax.broadcasted_iota(jnp.int32, (2 * PATCH, 1), 0)
    for b in range(ROWS // GROUP):
        part = slice(GROUP * b, GROUP * (b + 1))
        chosen[:, part] = jnp.where(position[0:1, part] == index, 1.0, 0.0).astype(BF16)
    for load in loads:
        load.wait()

    def own_patch(patch, carry):
        wait_all(outgoing.at[patch], arrived.at[patch], send_sem.at[patch], recv_sem.at[patch])
        attend(
            exact, arrived.at[patch], norm1_gain, norm1_shift, qkv_weight, proj,
            attended.at[patch], returned.at[patch], keys, query_t, value_t, mixed_t,
            send_sem.at[2 + patch], recv_sem.at[2 + patch],
        )
        return carry

    lax.fori_loop(0, 2, own_patch, 0)
    largest = jnp.zeros((1, C), F32)
    for patch in range(2):
        rows = from_wire(outgoing[patch])
        rows = jnp.where(rows[:, 0:1] < 0.5 * EMPTY, rows, 0.0)
        wait_all(
            attended.at[patch], returned.at[patch], send_sem.at[2 + patch], recv_sem.at[2 + patch]
        )
        back = from_wire(returned[patch])
        largest = jnp.maximum(largest, jnp.max(back, axis=0, keepdims=True))
        transform(rows, back, norm2_gain, norm2_shift, fc1, fc2, block_t)
        for b in range(ROWS // GROUP):
            part = slice(GROUP * b, GROUP * (b + 1))
            home = jnp.dot(
                block_t[...], chosen[PATCH * patch : PATCH * (patch + 1), part],
                preferred_element_type=F32,
            )
            if patch == 0:
                home_t[:, part] = home
            else:
                output[part, :] = (home_t[:, part] + home).astype(BF16).T
    marked[...] = jnp.where(largest[:, :1] > 0.1 * MARK, 1, 0)


VMEM = pl.BlockSpec(memory_space=pltpu.VMEM)
FAR = pl.BlockSpec(memory_space=pl.ANY)
WIRE = (2, DEVICES, 16, 128)


def fused(exact, *operands):
    return pl.pallas_call(
        functools.partial(block_kernel, exact),
        out_shape=(
            jax.ShapeDtypeStruct((ROWS, C), BF16),
            jax.ShapeDtypeStruct((1, 1), jnp.int32),
        ),
        in_specs=[FAR if i in (5, 11, 12, 15, 16) else VMEM for i in range(17)],
        out_specs=(VMEM, VMEM),
        scratch_shapes=[
            pltpu.VMEM((ROWS, C), BF16),
            pltpu.VMEM(WIRE, BF16),
            pltpu.VMEM(WIRE, BF16),
            pltpu.VMEM(WIRE, BF16),
            pltpu.VMEM(WIRE, BF16),
            pltpu.VMEM((1, ROWS), jnp.int32),
            pltpu.VMEM((C, 2048), BF16),
            pltpu.VMEM((KOFF, C, C), BF16),
            pltpu.VMEM((C, KOFF * C), BF16),
            pltpu.VMEM((KOFF, ROWS), jnp.int32),
            pltpu.VMEM((KOFF * C, GROUP), BF16),
            pltpu.VMEM((HB * BR, C), BF16),
            pltpu.VMEM((HB * BR, C), BF16),
            pltpu.VMEM((C, 3 * C), BF16),
            pltpu.VMEM((C, C), BF16),
            pltpu.VMEM((C, 4 * C), BF16),
            pltpu.VMEM((4 * C, C), BF16),
            pltpu.VMEM((PATCH, C), BF16),
            pltpu.VMEM((HEADS, 128, PATCH), BF16),
            pltpu.VMEM((HEADS, 2 * HEAD, PATCH), BF16),
            pltpu.VMEM((HEADS, HEAD, BLOCK), BF16),
            pltpu.VMEM((C, PATCH), BF16),
            pltpu.VMEM((C, ROWS), F32),
            pltpu.VMEM((2 * PATCH, ROWS), BF16),
            pltpu.SemaphoreType.DMA((6,)),
            pltpu.SemaphoreType.DMA((6,)),
            pltpu.SemaphoreType.DMA((5,)),
        ],
        compiler_params=pltpu.CompilerParams(
            collective_id=int(exact), has_side_effects=True, vmem_limit_bytes=58 * 2**20
        ),
        name="block_exact" if exact else "block",
    )(*operands)


def per_device(
    feats, nbr_brick, nbr_row, nbr_valid, dest, conv_weight, cpe_linear, cpe_gain, cpe_shift,
    norm1_gain, norm1_shift, qkv_weight, proj_weight, norm2_gain, norm2_shift, fc1_weight,
    fc2_weight,
):
    line = lambda v: v.reshape(1, C)
    operands = (
        feats, nbr_brick, nbr_row, nbr_valid, dest.reshape(1, ROWS), conv_weight, cpe_linear,
        line(cpe_gain), line(cpe_shift), line(norm1_gain), line(norm1_shift), qkv_weight,
        proj_weight, line(norm2_gain), line(norm2_shift), fc1_weight, fc2_weight,
    )
    output, marked = fused(False, *operands)
    return lax.cond(marked[0, 0] == 0, lambda: output, lambda: fused(True, *operands)[0])


def solution(mesh):
    placed = (
        P("space", None), P(None, "space"), P(None, "space"), P(None, "space"), P("space", None),
        P(), P(), P(), P(), P(), P(), P(), P(), P(), P(), P(), P(),
    )
    return jax.shard_map(
        per_device, mesh=mesh, in_specs=placed, out_specs=P("space", None), check_vma=False
    )
```

```python
import functools

import jax
import jax.numpy as jnp
from jax import lax
from jax.experimental import pallas as pl
from jax.experimental.pallas import tpu as pltpu
from jax.sharding import PartitionSpec as P

HEADS = 16
HEAD = 16
C = 256
PATCH = 1024
BR = 64
HB = 4
BLOCK = 512
KOFF = 27
DEVICES = 128
ROWS = 1536
GROUP = 256
WINDOW = 768
LOG2E = 1.4426950408889634
SAFE_SCORE = 60.0
EMPTY = 1024.0
MARK = 1e38
F32 = jnp.float32
BF16 = jnp.bfloat16


def layer_norm(values, gain, shift):
    average = jnp.mean(values, axis=-1, keepdims=True)
    centred = values - average
    spread = jnp.mean(centred * centred, axis=-1, keepdims=True)
    return centred * lax.rsqrt(spread + 1e-05) * gain + shift


def to_wire(rows):
    shaped = rows.reshape(rows.shape[0] // 8, 8, C)
    return jnp.concatenate([shaped[:, :, :128], shaped[:, :, 128:]], axis=1).astype(BF16)


def from_wire(block):
    wide = block.astype(F32)
    return jnp.concatenate([wide[:, :8], wide[:, 8:]], axis=2).reshape(PATCH, C)


def greet(barrier):
    me = lax.axis_index("space")

    def signal(step, carry):
        pl.semaphore_signal(
            barrier, inc=1, device_id=(lax.rem(me + step, DEVICES),),
            device_id_type=pl.DeviceIdType.MESH,
        )
        return carry

    lax.fori_loop(1, DEVICES, signal, 0)


def send_some(source, target, first, count, least, send_sem, recv_sem):
    me = lax.axis_index("space")

    def start(step, carry):
        other = first + lax.rem(me + step, count)
        pltpu.make_async_remote_copy(
            src_ref=source.at[other], dst_ref=target.at[me], send_sem=send_sem, recv_sem=recv_sem,
            device_id=(other,), device_id_type=pl.DeviceIdType.MESH,
        ).start()
        return carry

    lax.fori_loop(least, count, start, 0)


def keep_own(source, target, recv_sem):
    me = lax.axis_index("space")
    pltpu.make_async_copy(source.at[me], target.at[me], recv_sem).start()


def wait_all(source, target, send_sem, recv_sem):
    sent = source.at[pl.ds(0, DEVICES - 1)]
    pltpu.make_async_copy(sent, sent, send_sem).wait()
    pltpu.make_async_copy(target, target, recv_sem).wait()


def encode(
    feats, brick, row, valid, dest, weight, linear, gain, shift,
    enriched, outgoing, arrived, position,
    ext_t, weight_v, weight_t, relative, picked, low, high, is_home, send_sem, recv_sem, load_sem,
):
    me = lax.axis_index("space")
    barrier = pltpu.get_barrier_semaphore()
    loading = pltpu.make_async_copy(weight, weight_v, load_sem.at[0])
    loading.start()
    greet(barrier)

    own_t = HB * BR // GROUP
    for i in range(ROWS // GROUP):
        ext_t[:, GROUP * (i + own_t) : GROUP * (i + own_t + 1)] = feats[GROUP * i : GROUP * (i + 1), :].T

    base = lax.broadcasted_iota(jnp.int32, (KOFF, ROWS), 1) // GROUP * GROUP
    reach = brick[...] * BR + row[...]
    lowest = jnp.where(me == 0, HB * BR, 0)
    highest = jnp.where(me == DEVICES - 1, ROWS + HB * BR, ROWS + 2 * HB * BR)
    counted = (valid[...] > 0) & (reach >= lowest) & (reach < highest)
    relative[...] = jnp.where(counted, reach - base, -1)
    place = lax.broadcasted_iota(jnp.int16, (WINDOW // 16, 16, GROUP), 0) * 16 + (
        lax.broadcasted_iota(jnp.int16, (WINDOW // 16, 16, GROUP), 1)
    )

    def conv_group(g, turn):
        columns = pl.ds(pl.multiple_of(g * GROUP, GROUP), GROUP)
        window = ext_t[:, pl.ds(pl.multiple_of(g * GROUP, GROUP), WINDOW)]
        for k in range(KOFF):
            if turn:
                weight_t[:, C * k : C * (k + 1)] = weight_v[k].T
            wanted = jnp.broadcast_to(relative[k : k + 1, columns], (16, GROUP))
            chosen = jnp.where(
                wanted.astype(jnp.int16)[None] == place, BF16(1), BF16(0)
            ).reshape(WINDOW, GROUP)
            picked[C * k : C * (k + 1), :] = jnp.dot(
                window, chosen, preferred_element_type=F32
            ).astype(BF16)
        summed = jnp.dot(weight_t[...], picked[...], preferred_element_type=F32)
        convolved = summed.astype(BF16).T
        projected = jnp.dot(convolved, linear[...], preferred_element_type=F32)
        own = feats[columns, :].astype(F32)
        enriched[columns, :] = (own + layer_norm(projected, gain[...], shift[...])).astype(BF16)

    width = HB * BR
    up = pltpu.make_async_remote_copy(
        src_ref=feats.at[pl.ds(ROWS - width, width)], dst_ref=low, send_sem=send_sem.at[4],
        recv_sem=recv_sem.at[4], device_id=(lax.rem(me + 1, DEVICES),),
        device_id_type=pl.DeviceIdType.MESH,
    )
    down = pltpu.make_async_remote_copy(
        src_ref=feats.at[pl.ds(0, width)], dst_ref=high, send_sem=send_sem.at[5],
        recv_sem=recv_sem.at[5], device_id=(lax.rem(me + DEVICES - 1, DEVICES),),
        device_id_type=pl.DeviceIdType.MESH,
    )
    loading.wait()
    conv_group(1, True)
    pl.semaphore_wait(barrier, DEVICES - 1)
    up.start()
    down.start()

    def later_group(i, carry):
        @pl.when(i == 4)
        def _():
            up.wait()
            down.wait()
            ext_t[:, :GROUP] = low[...].T
            ext_t[:, ROWS + GROUP :] = high[...].T

        conv_group(jnp.where(i < 4, i + 1, (i - 4) * 5), False)
        return carry

    lax.fori_loop(1, ROWS // GROUP, later_group, 0)

    owner = lax.broadcasted_iota(jnp.int32, (128, 1), 0)
    before = jnp.where(
        lax.broadcasted_iota(jnp.int32, (GROUP, GROUP), 0)
        < lax.broadcasted_iota(jnp.int32, (GROUP, GROUP), 1), 1.0, 0.0,
    ).astype(BF16)
    count = jnp.zeros((128, 1), F32)
    for b in range(ROWS // GROUP):
        part = slice(GROUP * b, GROUP * (b + 1))
        target = dest[0:1, part]
        named = jnp.where(target == owner, 1.0, 0.0)
        running = jnp.dot(named.astype(BF16), before, preferred_element_type=F32) + count
        slot = jnp.sum(running * named, axis=0, keepdims=True).astype(jnp.int32)
        count = count + jnp.sum(named, axis=1, keepdims=True)
        position[0:1, part] = jnp.where(slot < 8, 0, PATCH) + target * 8 + slot % 8

    counts = jnp.broadcast_to(count, (128, 128)).astype(BF16)
    expand = jnp.where(
        lax.broadcasted_iota(jnp.int32, (PATCH, 128), 0) // 8
        == lax.broadcasted_iota(jnp.int32, (PATCH, 128), 1), 1.0, 0.0,
    ).astype(BF16)
    filled = jnp.dot(expand, counts, preferred_element_type=F32)
    filled = jnp.concatenate([filled, filled], axis=1)
    slots = (lax.broadcasted_iota(jnp.int32, (PATCH, C), 0) % 8).astype(F32)
    where_to = position[...]
    for patch in range(2):
        index = lax.broadcasted_iota(jnp.int32, (PATCH, 1), 0) + patch * PATCH
        chosen = jnp.where(index == where_to, 1.0, 0.0).astype(BF16)
        moved = jnp.dot(chosen, enriched[...], preferred_element_type=F32)
        outgoing[patch] = to_wire(jnp.where(slots + 8.0 * patch < filled, moved, EMPTY))
        send_some(
            outgoing.at[patch], arrived.at[patch], 0, DEVICES, 1, send_sem.at[patch],
            recv_sem.at[patch],
        )
        keep_own(outgoing.at[patch], arrived.at[patch], recv_sem.at[patch])
        if patch == 0:
            index = lax.broadcasted_iota(jnp.int32, (2 * PATCH, 1), 0)
            for b in range(ROWS // GROUP):
                part = slice(GROUP * b, GROUP * (b + 1))
                is_home[:, part] = jnp.where(where_to[:, part] == index, 1.0, 0.0).astype(BF16)


def attend(
    exact, arrived, gain, shift, qkv_weight, proj, attended, returned, keys, query_t, value_t,
    mixed_t, send_sem, recv_sem,
):
    rows = from_wire(arrived[...])
    occupied = rows[:, 0:1] < 0.5 * EMPTY
    rows = jnp.where(occupied, rows, 0.0)
    normed = layer_norm(rows, gain[...], shift[...]).astype(BF16)
    qkv = jnp.dot(normed, qkv_weight[...], preferred_element_type=F32).astype(BF16)
    queries = qkv[:, :C]
    keys[...] = qkv[:, C : 2 * C]
    values = jnp.where(occupied, qkv[:, 2 * C :], BF16(0))
    ones = jnp.broadcast_to(jnp.where(occupied, 1.0, 0.0), (PATCH, 128)).astype(BF16).T

    member = jnp.where(
        lax.broadcasted_iota(jnp.int32, (C, 128), 0) // HEAD
        == lax.broadcasted_iota(jnp.int32, (C, 128), 1), 1.0, 0.0,
    ).astype(BF16)

    def largest_square(table):
        wide = table.astype(F32)
        squares = jnp.dot((wide * wide).astype(BF16), member, preferred_element_type=F32)
        return jnp.max(squares, axis=0, keepdims=True)

    bound = jnp.max(
        largest_square(queries) * largest_square(qkv[:, C : 2 * C]), axis=1, keepdims=True
    ) / HEAD
    safe = bound < SAFE_SCORE * SAFE_SCORE

    turned = (queries * BF16(HEAD ** (-0.5))).T
    values_t = values.T
    channel = lax.broadcasted_iota(jnp.int32, (128, 1), 0) // HEAD
    for h in range(HEADS):
        half, inside = h // 8, h % 8
        query_t[h] = jnp.where(channel == inside, turned[128 * half : 128 * (half + 1), :], BF16(0))
        value_t[h, :HEAD] = values_t[HEAD * h : HEAD * (h + 1), :]
        value_t[h, HEAD:] = ones[:HEAD, :]

    penalty = jnp.where(occupied, 0.0, -1e30)

    def head(h, some, columns):
        scores = jnp.dot(some, query_t[h, :, columns], preferred_element_type=F32)
        if exact:
            scores = jnp.where(penalty < 0.0, penalty, scores)
            scores = scores - jnp.max(scores, axis=0, keepdims=True)
        weights = jnp.exp2(scores * LOG2E).astype(BF16)
        products = jnp.dot(value_t[h], weights, preferred_element_type=F32)
        below = products[HEAD : HEAD + 1, :]
        below = jnp.where(below > 0, below, 1.0)
        return (products[:HEAD, :] / below).astype(BF16)

    me = lax.axis_index("space")
    near = BLOCK // 8

    def some_queries(turn, carry):
        block = lax.rem(me // near + turn, PATCH // BLOCK)
        start = pl.multiple_of(block * BLOCK, BLOCK)

        if exact:
            def one_head(t, carry):
                h, offset = t // (BLOCK // 128), t % (BLOCK // 128) * 128
                some = keys[:, pl.ds(pl.multiple_of(h // 8 * 128, 128), 128)]
                mixed_t[h, :, pl.ds(pl.multiple_of(offset, 128), 128)] = head(
                    h, some, pl.ds(pl.multiple_of(start + offset, 128), 128)
                )
                return carry

            lax.fori_loop(0, HEADS * (BLOCK // 128), one_head, 0)
        else:
            for h in range(HEADS):
                some = keys[:, h // 8 * 128 : h // 8 * 128 + 128]
                mixed_t[h] = head(h, some, pl.ds(start, BLOCK))

        mixed = mixed_t[...].reshape(C, BLOCK).T
        result = jnp.dot(mixed, proj[...], preferred_element_type=F32)
        if not exact:
            result = jnp.where(jnp.broadcast_to(safe, (BLOCK, 1)), result, MARK)
        first = pl.multiple_of(block * near, near)
        attended[pl.ds(first, near)] = to_wire(result)

        @pl.when(turn == 0)
        def _():
            keep_own(attended, returned, recv_sem)

        send_some(
            attended, returned, first, near, jnp.where(turn == 0, 1, 0), send_sem, recv_sem
        )
        return carry

    lax.fori_loop(0, PATCH // BLOCK, some_queries, 0)


def transform(rows, attended, gain, shift, fc1, fc2, block_t):
    for b in range(PATCH // GROUP):
        part = slice(GROUP * b, GROUP * (b + 1))
        residual = rows[part] + attended[part]
        normed = layer_norm(residual, gain[...], shift[...]).astype(BF16)
        inner = jnp.dot(normed, fc1[...], preferred_element_type=F32)
        hidden = (0.5 * inner * (1.0 + lax.erf(inner * (0.5 ** 0.5)))).astype(BF16)
        finished = residual + jnp.dot(hidden, fc2[...], preferred_element_type=F32)
        block_t[:, part] = finished.astype(BF16).T


def block_kernel(
    exact,
    feats, brick, row, valid, dest, weight, linear, cpe_gain, cpe_shift, norm1_gain, norm1_shift,
    qkv_far, proj_far, norm2_gain, norm2_shift, fc1_far, fc2_far,
    output, marked,
    enriched, outgoing, arrived, attended, returned, position,
    ext_t, weight_v, weight_t, relative, picked, low, high, qkv_weight, proj, fc1, fc2,
    keys, query_t, value_t, mixed_t, block_t, home_t, chosen, send_sem, recv_sem, load_sem,
):
    loads = [
        pltpu.make_async_copy(far, near, load_sem.at[1 + i])
        for i, (far, near) in enumerate(
            ((qkv_far, qkv_weight), (proj_far, proj), (fc1_far, fc1), (fc2_far, fc2))
        )
    ]
    for load in loads:
        load.start()
    encode(
        feats, brick, row, valid, dest, weight, linear, cpe_gain, cpe_shift,
        enriched, outgoing, arrived, position,
        ext_t, weight_v, weight_t, relative, picked, low, high, chosen, send_sem, recv_sem, load_sem,
    )
    for load in loads:
        load.wait()

    def own_patch(patch, carry):
        wait_all(outgoing.at[patch], arrived.at[patch], send_sem.at[patch], recv_sem.at[patch])
        attend(
            exact, arrived.at[patch], norm1_gain, norm1_shift, qkv_weight, proj,
            attended.at[patch], returned.at[patch], keys, query_t, value_t, mixed_t,
            send_sem.at[2 + patch], recv_sem.at[2 + patch],
        )
        return carry

    lax.fori_loop(0, 2, own_patch, 0)
    largest = jnp.zeros((1, C), F32)
    for patch in range(2):
        rows = from_wire(outgoing[patch])
        rows = jnp.where(rows[:, 0:1] < 0.5 * EMPTY, rows, 0.0)
        wait_all(
            attended.at[patch], returned.at[patch], send_sem.at[2 + patch], recv_sem.at[2 + patch]
        )
        back = from_wire(returned[patch])
        largest = jnp.maximum(largest, jnp.max(back, axis=0, keepdims=True))
        transform(rows, back, norm2_gain, norm2_shift, fc1, fc2, block_t)
        for b in range(ROWS // GROUP):
            part = slice(GROUP * b, GROUP * (b + 1))
            home = jnp.dot(
                block_t[...], chosen[PATCH * patch : PATCH * (patch + 1), part],
                preferred_element_type=F32,
            )
            if patch == 0:
                home_t[:, part] = home
            else:
                output[part, :] = (home_t[:, part] + home).astype(BF16).T
    marked[...] = jnp.where(largest[:, :1] > 0.1 * MARK, 1, 0)


VMEM = pl.BlockSpec(memory_space=pltpu.VMEM)
FAR = pl.BlockSpec(memory_space=pl.ANY)
WIRE = (2, DEVICES, 16, 128)


def fused(exact, *operands):
    return pl.pallas_call(
        functools.partial(block_kernel, exact),
        out_shape=(
            jax.ShapeDtypeStruct((ROWS, C), BF16),
            jax.ShapeDtypeStruct((1, 1), jnp.int32),
        ),
        in_specs=[FAR if i in (5, 11, 12, 15, 16) else VMEM for i in range(17)],
        out_specs=(VMEM, VMEM),
        scratch_shapes=[
            pltpu.VMEM((ROWS, C), BF16),
            pltpu.VMEM(WIRE, BF16),
            pltpu.VMEM(WIRE, BF16),
            pltpu.VMEM(WIRE, BF16),
            pltpu.VMEM(WIRE, BF16),
            pltpu.VMEM((1, ROWS), jnp.int32),
            pltpu.VMEM((C, 2048), BF16),
            pltpu.VMEM((KOFF, C, C), BF16),
            pltpu.VMEM((C, KOFF * C), BF16),
            pltpu.VMEM((KOFF, ROWS), jnp.int32),
            pltpu.VMEM((KOFF * C, GROUP), BF16),
            pltpu.VMEM((HB * BR, C), BF16),
            pltpu.VMEM((HB * BR, C), BF16),
            pltpu.VMEM((C, 3 * C), BF16),
            pltpu.VMEM((C, C), BF16),
            pltpu.VMEM((C, 4 * C), BF16),
            pltpu.VMEM((4 * C, C), BF16),
            pltpu.VMEM((PATCH, C), BF16),
            pltpu.VMEM((HEADS, 128, PATCH), BF16),
            pltpu.VMEM((HEADS, 2 * HEAD, PATCH), BF16),
            pltpu.VMEM((HEADS, HEAD, BLOCK), BF16),
            pltpu.VMEM((C, PATCH), BF16),
            pltpu.VMEM((C, ROWS), F32),
            pltpu.VMEM((2 * PATCH, ROWS), BF16),
            pltpu.SemaphoreType.DMA((6,)),
            pltpu.SemaphoreType.DMA((6,)),
            pltpu.SemaphoreType.DMA((5,)),
        ],
        compiler_params=pltpu.CompilerParams(
            collective_id=int(exact), has_side_effects=True, vmem_limit_bytes=58 * 2**20
        ),
        name="block_exact" if exact else "block",
    )(*operands)


def per_device(
    feats, nbr_brick, nbr_row, nbr_valid, dest, conv_weight, cpe_linear, cpe_gain, cpe_shift,
    norm1_gain, norm1_shift, qkv_weight, proj_weight, norm2_gain, norm2_shift, fc1_weight,
    fc2_weight,
):
    line = lambda v: v.reshape(1, C)
    operands = (
        feats, nbr_brick, nbr_row, nbr_valid, dest.reshape(1, ROWS), conv_weight, cpe_linear,
        line(cpe_gain), line(cpe_shift), line(norm1_gain), line(norm1_shift), qkv_weight,
        proj_weight, line(norm2_gain), line(norm2_shift), fc1_weight, fc2_weight,
    )
    output, marked = fused(False, *operands)
    return lax.cond(marked[0, 0] == 0, lambda: output, lambda: fused(True, *operands)[0])


def solution(mesh):
    placed = (
        P("space", None), P(None, "space"), P(None, "space"), P(None, "space"), P("space", None),
        P(), P(), P(), P(), P(), P(), P(), P(), P(), P(), P(), P(),
    )
    return jax.shard_map(
        per_device, mesh=mesh, in_specs=placed, out_specs=P("space", None), check_vma=False
    )
```

```python
import functools

import jax
import jax.numpy as jnp
from jax import lax
from jax.experimental import pallas as pl
from jax.experimental.pallas import tpu as pltpu
from jax.sharding import PartitionSpec as P

HEADS = 16
HEAD = 16
C = 256
PATCH = 1024
BR = 64
HB = 4
BLOCK = 512
KOFF = 27
DEVICES = 128
ROWS = 1536
GROUP = 256
WINDOW = 768
LOG2E = 1.4426950408889634
SAFE_SCORE = 60.0
EMPTY = 1024.0
MARK = 1e38
F32 = jnp.float32
BF16 = jnp.bfloat16


def layer_norm(values, gain, shift):
    average = jnp.mean(values, axis=-1, keepdims=True)
    centred = values - average
    spread = jnp.mean(centred * centred, axis=-1, keepdims=True)
    return centred * lax.rsqrt(spread + 1e-05) * gain + shift


def to_wire(rows):
    shaped = rows.reshape(rows.shape[0] // 8, 8, C)
    return jnp.concatenate([shaped[:, :, :128], shaped[:, :, 128:]], axis=1).astype(BF16)


def from_wire(block):
    wide = block.astype(F32)
    return jnp.concatenate([wide[:, :8], wide[:, 8:]], axis=2).reshape(PATCH, C)


def greet(barrier):
    me = lax.axis_index("space")

    def signal(step, carry):
        pl.semaphore_signal(
            barrier, inc=1, device_id=(lax.rem(me + step, DEVICES),),
            device_id_type=pl.DeviceIdType.MESH,
        )
        return carry

    lax.fori_loop(1, DEVICES, signal, 0)


def send_some(source, target, first, count, least, send_sem, recv_sem):
    me = lax.axis_index("space")

    def start(step, carry):
        other = first + lax.rem(me + step, count)
        pltpu.make_async_remote_copy(
            src_ref=source.at[other], dst_ref=target.at[me], send_sem=send_sem, recv_sem=recv_sem,
            device_id=(other,), device_id_type=pl.DeviceIdType.MESH,
        ).start()
        return carry

    lax.fori_loop(least, count, start, 0)


def keep_own(source, target, recv_sem):
    me = lax.axis_index("space")
    pltpu.make_async_copy(source.at[me], target.at[me], recv_sem).start()


def wait_all(source, target, send_sem, recv_sem):
    sent = source.at[pl.ds(0, DEVICES - 1)]
    pltpu.make_async_copy(sent, sent, send_sem).wait()
    pltpu.make_async_copy(target, target, recv_sem).wait()


def encode(
    exact, feats, brick, row, valid, dest, weight, linear, gain, shift,
    enriched, outgoing, arrived, position,
    ext_t, weight_v, weight_t, relative, picked, low, high, is_home, send_sem, recv_sem, load_sem,
):
    me = lax.axis_index("space")
    barrier = pltpu.get_barrier_semaphore()
    loading = pltpu.make_async_copy(weight, weight_v, load_sem.at[0])
    loading.start()
    greet(barrier)

    own_t = HB * BR // GROUP
    for i in range(ROWS // GROUP):
        ext_t[:, GROUP * (i + own_t) : GROUP * (i + own_t + 1)] = feats[GROUP * i : GROUP * (i + 1), :].T

    base = lax.broadcasted_iota(jnp.int32, (KOFF, ROWS), 1) // GROUP * GROUP
    reach = brick[...] * BR + row[...]
    lowest = jnp.where(me == 0, HB * BR, 0)
    highest = jnp.where(me == DEVICES - 1, ROWS + HB * BR, ROWS + 2 * HB * BR)
    counted = (valid[...] > 0) & (reach >= lowest) & (reach < highest)
    relative[...] = jnp.where(counted, reach - base, -1)
    place = lax.broadcasted_iota(jnp.int16, (WINDOW // 16, 16, GROUP), 0) * 16 + (
        lax.broadcasted_iota(jnp.int16, (WINDOW // 16, 16, GROUP), 1)
    )

    def conv_group(g, turn):
        columns = pl.ds(pl.multiple_of(g * GROUP, GROUP), GROUP)
        window = ext_t[:, pl.ds(pl.multiple_of(g * GROUP, GROUP), WINDOW)]
        for k in range(KOFF):
            if turn:
                weight_t[:, C * k : C * (k + 1)] = weight_v[k].T
            wanted = jnp.broadcast_to(relative[k : k + 1, columns], (16, GROUP))
            chosen = jnp.where(
                wanted.astype(jnp.int16)[None] == place, BF16(1), BF16(0)
            ).reshape(WINDOW, GROUP)
            picked[C * k : C * (k + 1), :] = jnp.dot(
                window, chosen, preferred_element_type=F32
            ).astype(BF16)
        summed = jnp.dot(weight_t[...], picked[...], preferred_element_type=F32)
        convolved = summed.astype(BF16).T
        projected = jnp.dot(convolved, linear[...], preferred_element_type=F32)
        own = feats[columns, :].astype(F32)
        enriched[columns, :] = (own + layer_norm(projected, gain[...], shift[...])).astype(BF16)

    width = HB * BR
    up = pltpu.make_async_remote_copy(
        src_ref=feats.at[pl.ds(ROWS - width, width)], dst_ref=low, send_sem=send_sem.at[4],
        recv_sem=recv_sem.at[4], device_id=(lax.rem(me + 1, DEVICES),),
        device_id_type=pl.DeviceIdType.MESH,
    )
    down = pltpu.make_async_remote_copy(
        src_ref=feats.at[pl.ds(0, width)], dst_ref=high, send_sem=send_sem.at[5],
        recv_sem=recv_sem.at[5], device_id=(lax.rem(me + DEVICES - 1, DEVICES),),
        device_id_type=pl.DeviceIdType.MESH,
    )
    loading.wait()
    if exact:

        def turn_weight(k, carry):
            weight_t[:, pl.ds(pl.multiple_of(k * C, C), C)] = weight_v[k].T
            return carry

        lax.fori_loop(0, KOFF, turn_weight, 0)
    else:
        conv_group(1, True)
    pl.semaphore_wait(barrier, DEVICES - 1)
    up.start()
    down.start()

    def later_group(i, carry):
        @pl.when(i == 4)
        def _():
            up.wait()
            down.wait()
            ext_t[:, :GROUP] = low[...].T
            ext_t[:, ROWS + GROUP :] = high[...].T

        conv_group(jnp.where(i < 4, i + 1, (i - 4) * 5), False)
        return carry

    lax.fori_loop(0 if exact else 1, ROWS // GROUP, later_group, 0)

    owner = lax.broadcasted_iota(jnp.int32, (128, 1), 0)
    before = jnp.where(
        lax.broadcasted_iota(jnp.int32, (GROUP, GROUP), 0)
        < lax.broadcasted_iota(jnp.int32, (GROUP, GROUP), 1), 1.0, 0.0,
    ).astype(BF16)
    count = jnp.zeros((128, 1), F32)
    for b in range(ROWS // GROUP):
        part = slice(GROUP * b, GROUP * (b + 1))
        target = dest[0:1, part]
        named = jnp.where(target == owner, 1.0, 0.0)
        running = jnp.dot(named.astype(BF16), before, preferred_element_type=F32) + count
        slot = jnp.sum(running * named, axis=0, keepdims=True).astype(jnp.int32)
        count = count + jnp.sum(named, axis=1, keepdims=True)
        position[0:1, part] = jnp.where(slot < 8, 0, PATCH) + target * 8 + slot % 8

    counts = jnp.broadcast_to(count, (128, 128)).astype(BF16)
    expand = jnp.where(
        lax.broadcasted_iota(jnp.int32, (PATCH, 128), 0) // 8
        == lax.broadcasted_iota(jnp.int32, (PATCH, 128), 1), 1.0, 0.0,
    ).astype(BF16)
    filled = jnp.dot(expand, counts, preferred_element_type=F32)
    filled = jnp.concatenate([filled, filled], axis=1)
    slots = (lax.broadcasted_iota(jnp.int32, (PATCH, C), 0) % 8).astype(F32)
    where_to = position[...]
    for patch in range(2):
        index = lax.broadcasted_iota(jnp.int32, (PATCH, 1), 0) + patch * PATCH
        chosen = jnp.where(index == where_to, 1.0, 0.0).astype(BF16)
        moved = jnp.dot(chosen, enriched[...], preferred_element_type=F32)
        outgoing[patch] = to_wire(jnp.where(slots + 8.0 * patch < filled, moved, EMPTY))
        send_some(
            outgoing.at[patch], arrived.at[patch], 0, DEVICES, 1, send_sem.at[patch],
            recv_sem.at[patch],
        )
        keep_own(outgoing.at[patch], arrived.at[patch], recv_sem.at[patch])
        if patch == 0:
            index = lax.broadcasted_iota(jnp.int32, (2 * PATCH, 1), 0)
            for b in range(ROWS // GROUP):
                part = slice(GROUP * b, GROUP * (b + 1))
                is_home[:, part] = jnp.where(where_to[:, part] == index, 1.0, 0.0).astype(BF16)


def attend(
    exact, arrived, gain, shift, qkv_weight, proj, attended, returned, keys, query_t, value_t,
    mixed_t, send_sem, recv_sem,
):
    rows = from_wire(arrived[...])
    occupied = rows[:, 0:1] < 0.5 * EMPTY
    rows = jnp.where(occupied, rows, 0.0)
    normed = layer_norm(rows, gain[...], shift[...]).astype(BF16)
    qkv = jnp.dot(normed, qkv_weight[...], preferred_element_type=F32).astype(BF16)
    queries = qkv[:, :C]
    keys[...] = qkv[:, C : 2 * C]
    values = jnp.where(occupied, qkv[:, 2 * C :], BF16(0))
    ones = jnp.broadcast_to(jnp.where(occupied, 1.0, 0.0), (PATCH, 128)).astype(BF16).T

    member = jnp.where(
        lax.broadcasted_iota(jnp.int32, (C, 128), 0) // HEAD
        == lax.broadcasted_iota(jnp.int32, (C, 128), 1), 1.0, 0.0,
    ).astype(BF16)

    def largest_square(table):
        wide = table.astype(F32)
        squares = jnp.dot((wide * wide).astype(BF16), member, preferred_element_type=F32)
        return jnp.max(squares, axis=0, keepdims=True)

    bound = jnp.max(
        largest_square(queries) * largest_square(qkv[:, C : 2 * C]), axis=1, keepdims=True
    ) / HEAD
    safe = bound < SAFE_SCORE * SAFE_SCORE

    turned = (queries * BF16(HEAD ** (-0.5))).T
    values_t = values.T
    channel = lax.broadcasted_iota(jnp.int32, (128, 1), 0) // HEAD
    for h in range(HEADS):
        half, inside = h // 8, h % 8
        query_t[h] = jnp.where(channel == inside, turned[128 * half : 128 * (half + 1), :], BF16(0))
        value_t[h, :HEAD] = values_t[HEAD * h : HEAD * (h + 1), :]
        value_t[h, HEAD:] = ones[:HEAD, :]

    penalty = jnp.where(occupied, 0.0, -1e30)

    def head(h, some, columns):
        scores = jnp.dot(some, query_t[h, :, columns], preferred_element_type=F32)
        if exact:
            scores = jnp.where(penalty < 0.0, penalty, scores)
            scores = scores - jnp.max(scores, axis=0, keepdims=True)
        weights = jnp.exp2(scores * LOG2E).astype(BF16)
        products = jnp.dot(value_t[h], weights, preferred_element_type=F32)
        below = products[HEAD : HEAD + 1, :]
        below = jnp.where(below > 0, below, 1.0)
        return (products[:HEAD, :] / below).astype(BF16)

    me = lax.axis_index("space")
    near = BLOCK // 8

    def some_queries(turn, carry):
        block = lax.rem(me // near + turn, PATCH // BLOCK)
        start = pl.multiple_of(block * BLOCK, BLOCK)

        if exact:
            def one_head(t, carry):
                h, offset = t // (BLOCK // 128), t % (BLOCK // 128) * 128
                some = keys[:, pl.ds(pl.multiple_of(h // 8 * 128, 128), 128)]
                mixed_t[h, :, pl.ds(pl.multiple_of(offset, 128), 128)] = head(
                    h, some, pl.ds(pl.multiple_of(start + offset, 128), 128)
                )
                return carry

            lax.fori_loop(0, HEADS * (BLOCK // 128), one_head, 0)
        else:
            for h in range(HEADS):
                some = keys[:, h // 8 * 128 : h // 8 * 128 + 128]
                mixed_t[h] = head(h, some, pl.ds(start, BLOCK))

        mixed = mixed_t[...].reshape(C, BLOCK).T
        result = jnp.dot(mixed, proj[...], preferred_element_type=F32)
        if not exact:
            result = jnp.where(jnp.broadcast_to(safe, (BLOCK, 1)), result, MARK)
        first = pl.multiple_of(block * near, near)
        attended[pl.ds(first, near)] = to_wire(result)

        @pl.when(turn == 0)
        def _():
            keep_own(attended, returned, recv_sem)

        send_some(
            attended, returned, first, near, jnp.where(turn == 0, 1, 0), send_sem, recv_sem
        )
        return carry

    lax.fori_loop(0, PATCH // BLOCK, some_queries, 0)


def transform(rows, attended, gain, shift, fc1, fc2, block_t):
    def some_rows(rows, attended):
        residual = rows + attended
        normed = layer_norm(residual, gain[...], shift[...]).astype(BF16)
        inner = jnp.dot(normed, fc1[...], preferred_element_type=F32)
        hidden = (0.5 * inner * (1.0 + lax.erf(inner * (0.5 ** 0.5)))).astype(BF16)
        return residual + jnp.dot(hidden, fc2[...], preferred_element_type=F32)

    for b in range(PATCH // GROUP):
        part = slice(GROUP * b, GROUP * (b + 1))
        block_t[:, part] = some_rows(rows[part], attended[part]).astype(BF16).T


def block_kernel(
    exact,
    feats, brick, row, valid, dest, weight, linear, cpe_gain, cpe_shift, norm1_gain, norm1_shift,
    qkv_far, proj_far, norm2_gain, norm2_shift, fc1_far, fc2_far,
    output, marked,
    enriched, outgoing, arrived, attended, returned, position,
    ext_t, weight_v, weight_t, relative, picked, low, high, qkv_weight, proj, fc1, fc2,
    keys, query_t, value_t, mixed_t, block_t, home_t, chosen, send_sem, recv_sem, load_sem,
):
    loads = [
        pltpu.make_async_copy(far, near, load_sem.at[1 + i])
        for i, (far, near) in enumerate(
            ((qkv_far, qkv_weight), (proj_far, proj), (fc1_far, fc1), (fc2_far, fc2))
        )
    ]
    for load in loads:
        load.start()
    encode(
        exact, feats, brick, row, valid, dest, weight, linear, cpe_gain, cpe_shift,
        enriched, outgoing, arrived, position,
        ext_t, weight_v, weight_t, relative, picked, low, high, chosen, send_sem, recv_sem, load_sem,
    )
    for load in loads:
        load.wait()

    def own_patch(patch, carry):
        wait_all(outgoing.at[patch], arrived.at[patch], send_sem.at[patch], recv_sem.at[patch])
        attend(
            exact, arrived.at[patch], norm1_gain, norm1_shift, qkv_weight, proj,
            attended.at[patch], returned.at[patch], keys, query_t, value_t, mixed_t,
            send_sem.at[2 + patch], recv_sem.at[2 + patch],
        )
        return carry

    lax.fori_loop(0, 2, own_patch, 0)
    def give_back(patch):
        rows = from_wire(outgoing[patch])
        rows = jnp.where(rows[:, 0:1] < 0.5 * EMPTY, rows, 0.0)
        wait_all(
            attended.at[patch], returned.at[patch], send_sem.at[2 + patch], recv_sem.at[2 + patch]
        )
        back = from_wire(returned[patch])
        transform(rows, back, norm2_gain, norm2_shift, fc1, fc2, block_t)
        return jnp.max(back, axis=0, keepdims=True)

    parts = [slice(GROUP * b, GROUP * (b + 1)) for b in range(ROWS // GROUP)]
    if exact:
        home_t[...] = jnp.zeros((C, ROWS), F32)

        def add_patch(patch, carry):
            give_back(patch)
            own = pl.ds(pl.multiple_of(patch * PATCH, PATCH), PATCH)
            for part in parts:
                home_t[:, part] += jnp.dot(
                    block_t[...], chosen[own, part], preferred_element_type=F32
                )
            return carry

        lax.fori_loop(0, 2, add_patch, 0)
        for part in parts:
            output[part, :] = home_t[:, part].astype(BF16).T
        marked[...] = jnp.zeros((1, 1), jnp.int32)
        return

    largest = jnp.zeros((1, C), F32)
    for patch in range(2):
        largest = jnp.maximum(largest, give_back(patch))
        for part in parts:
            home = jnp.dot(
                block_t[...], chosen[PATCH * patch : PATCH * (patch + 1), part],
                preferred_element_type=F32,
            )
            if patch == 0:
                home_t[:, part] = home
            else:
                output[part, :] = (home_t[:, part] + home).astype(BF16).T
    marked[...] = jnp.where(largest[:, :1] > 0.1 * MARK, 1, 0)


VMEM = pl.BlockSpec(memory_space=pltpu.VMEM)
FAR = pl.BlockSpec(memory_space=pl.ANY)
WIRE = (2, DEVICES, 16, 128)


def fused(exact, *operands):
    return pl.pallas_call(
        functools.partial(block_kernel, exact),
        out_shape=(
            jax.ShapeDtypeStruct((ROWS, C), BF16),
            jax.ShapeDtypeStruct((1, 1), jnp.int32),
        ),
        in_specs=[FAR if i in (5, 11, 12, 15, 16) else VMEM for i in range(17)],
        out_specs=(VMEM, VMEM),
        scratch_shapes=[
            pltpu.VMEM((ROWS, C), BF16),
            pltpu.VMEM(WIRE, BF16),
            pltpu.VMEM(WIRE, BF16),
            pltpu.VMEM(WIRE, BF16),
            pltpu.VMEM(WIRE, BF16),
            pltpu.VMEM((1, ROWS), jnp.int32),
            pltpu.VMEM((C, 2048), BF16),
            pltpu.VMEM((KOFF, C, C), BF16),
            pltpu.VMEM((C, KOFF * C), BF16),
            pltpu.VMEM((KOFF, ROWS), jnp.int32),
            pltpu.VMEM((KOFF * C, GROUP), BF16),
            pltpu.VMEM((HB * BR, C), BF16),
            pltpu.VMEM((HB * BR, C), BF16),
            pltpu.VMEM((C, 3 * C), BF16),
            pltpu.VMEM((C, C), BF16),
            pltpu.VMEM((C, 4 * C), BF16),
            pltpu.VMEM((4 * C, C), BF16),
            pltpu.VMEM((PATCH, C), BF16),
            pltpu.VMEM((HEADS, 128, PATCH), BF16),
            pltpu.VMEM((HEADS, 2 * HEAD, PATCH), BF16),
            pltpu.VMEM((HEADS, HEAD, BLOCK), BF16),
            pltpu.VMEM((C, PATCH), BF16),
            pltpu.VMEM((C, ROWS), F32),
            pltpu.VMEM((2 * PATCH, ROWS), BF16),
            pltpu.SemaphoreType.DMA((6,)),
            pltpu.SemaphoreType.DMA((6,)),
            pltpu.SemaphoreType.DMA((5,)),
        ],
        compiler_params=pltpu.CompilerParams(
            collective_id=int(exact), has_side_effects=True, vmem_limit_bytes=58 * 2**20
        ),
        name="block_exact" if exact else "block",
    )(*operands)


def per_device(
    feats, nbr_brick, nbr_row, nbr_valid, dest, conv_weight, cpe_linear, cpe_gain, cpe_shift,
    norm1_gain, norm1_shift, qkv_weight, proj_weight, norm2_gain, norm2_shift, fc1_weight,
    fc2_weight,
):
    line = lambda v: v.reshape(1, C)
    operands = (
        feats, nbr_brick, nbr_row, nbr_valid, dest.reshape(1, ROWS), conv_weight, cpe_linear,
        line(cpe_gain), line(cpe_shift), line(norm1_gain), line(norm1_shift), qkv_weight,
        proj_weight, line(norm2_gain), line(norm2_shift), fc1_weight, fc2_weight,
    )
    output, marked = fused(False, *operands)
    return lax.cond(marked[0, 0] == 0, lambda: output, lambda: fused(True, *operands)[0])


def solution(mesh):
    placed = (
        P("space", None), P(None, "space"), P(None, "space"), P(None, "space"), P("space", None),
        P(), P(), P(), P(), P(), P(), P(), P(), P(), P(), P(), P(),
    )
    return jax.shard_map(
        per_device, mesh=mesh, in_specs=placed, out_specs=P("space", None), check_vma=False
    )
```

```python
import functools

import jax
import jax.numpy as jnp
from jax import lax
from jax.experimental import pallas as pl
from jax.experimental.pallas import tpu as pltpu
from jax.sharding import PartitionSpec as P

HEADS = 16
HEAD = 16
C = 256
PATCH = 1024
BR = 64
HB = 4
BLOCK = 512
KOFF = 27
DEVICES = 128
ROWS = 1536
GROUP = 256
WINDOW = 768
LOG2E = 1.4426950408889634
SAFE_SCORE = 60.0
EMPTY = 1024.0
MARK = 1e38
F32 = jnp.float32
BF16 = jnp.bfloat16


def layer_norm(values, gain, shift):
    average = jnp.mean(values, axis=-1, keepdims=True)
    centred = values - average
    spread = jnp.mean(centred * centred, axis=-1, keepdims=True)
    return centred * lax.rsqrt(spread + 1e-05) * gain + shift


def to_wire(rows):
    shaped = rows.reshape(rows.shape[0] // 8, 8, C)
    return jnp.concatenate([shaped[:, :, :128], shaped[:, :, 128:]], axis=1).astype(BF16)


def from_wire(block):
    wide = block.astype(F32)
    return jnp.concatenate([wide[:, :8], wide[:, 8:]], axis=2).reshape(PATCH, C)


def greet(barrier):
    me = lax.axis_index("space")

    def signal(step, carry):
        pl.semaphore_signal(
            barrier, inc=1, device_id=(lax.rem(me + step, DEVICES),),
            device_id_type=pl.DeviceIdType.MESH,
        )
        return carry

    lax.fori_loop(1, DEVICES, signal, 0)


def send_some(source, target, first, count, least, send_sem, recv_sem):
    me = lax.axis_index("space")

    def start(step, carry):
        other = first + lax.rem(me + step, count)
        pltpu.make_async_remote_copy(
            src_ref=source.at[other], dst_ref=target.at[me], send_sem=send_sem, recv_sem=recv_sem,
            device_id=(other,), device_id_type=pl.DeviceIdType.MESH,
        ).start()
        return carry

    lax.fori_loop(least, count, start, 0)


def keep_own(source, target, recv_sem):
    me = lax.axis_index("space")
    pltpu.make_async_copy(source.at[me], target.at[me], recv_sem).start()


def wait_all(source, target, send_sem, recv_sem):
    sent = source.at[pl.ds(0, DEVICES - 1)]
    pltpu.make_async_copy(sent, sent, send_sem).wait()
    pltpu.make_async_copy(target, target, recv_sem).wait()


def encode(
    feats, brick, row, valid, dest, weight, linear, gain, shift,
    enriched, outgoing, arrived, position,
    ext_t, weight_v, weight_t, relative, picked, low, high, send_sem, recv_sem, load_sem,
):
    me = lax.axis_index("space")
    barrier = pltpu.get_barrier_semaphore()
    loading = pltpu.make_async_copy(weight, weight_v, load_sem.at[0])
    loading.start()
    greet(barrier)

    own_t = HB * BR // GROUP
    for i in range(ROWS // GROUP):
        ext_t[:, GROUP * (i + own_t) : GROUP * (i + own_t + 1)] = feats[GROUP * i : GROUP * (i + 1), :].T

    base = lax.broadcasted_iota(jnp.int32, (KOFF, ROWS), 1) // GROUP * GROUP
    reach = brick[...] * BR + row[...]
    lowest = jnp.where(me == 0, HB * BR, 0)
    highest = jnp.where(me == DEVICES - 1, ROWS + HB * BR, ROWS + 2 * HB * BR)
    counted = (valid[...] > 0) & (reach >= lowest) & (reach < highest)
    relative[...] = jnp.where(counted, reach - base, -1)
    place = lax.broadcasted_iota(jnp.int32, (WINDOW, 1), 0)

    def conv_group(g, turn):
        columns = pl.ds(pl.multiple_of(g * GROUP, GROUP), GROUP)
        window = ext_t[:, pl.ds(pl.multiple_of(g * GROUP, GROUP), WINDOW)]
        for k in range(KOFF):
            if turn:
                weight_t[:, C * k : C * (k + 1)] = weight_v[k].T
            chosen = jnp.where(relative[k : k + 1, columns] == place, 1.0, 0.0).astype(BF16)
            picked[C * k : C * (k + 1), :] = jnp.dot(
                window, chosen, preferred_element_type=F32
            ).astype(BF16)
        summed = jnp.dot(weight_t[...], picked[...], preferred_element_type=F32)
        convolved = summed.astype(BF16).T
        projected = jnp.dot(convolved, linear[...], preferred_element_type=F32)
        own = feats[columns, :].astype(F32)
        enriched[columns, :] = (own + layer_norm(projected, gain[...], shift[...])).astype(BF16)

    width = HB * BR
    up = pltpu.make_async_remote_copy(
        src_ref=feats.at[pl.ds(ROWS - width, width)], dst_ref=low, send_sem=send_sem.at[4],
        recv_sem=recv_sem.at[4], device_id=(lax.rem(me + 1, DEVICES),),
        device_id_type=pl.DeviceIdType.MESH,
    )
    down = pltpu.make_async_remote_copy(
        src_ref=feats.at[pl.ds(0, width)], dst_ref=high, send_sem=send_sem.at[5],
        recv_sem=recv_sem.at[5], device_id=(lax.rem(me + DEVICES - 1, DEVICES),),
        device_id_type=pl.DeviceIdType.MESH,
    )
    loading.wait()
    conv_group(1, True)
    pl.semaphore_wait(barrier, DEVICES - 1)
    up.start()
    down.start()

    def later_group(i, carry):
        @pl.when(i == 4)
        def _():
            up.wait()
            down.wait()
            ext_t[:, :GROUP] = low[...].T
            ext_t[:, ROWS + GROUP :] = high[...].T

        conv_group(jnp.where(i < 4, i + 1, (i - 4) * 5), False)
        return carry

    lax.fori_loop(1, ROWS // GROUP, later_group, 0)

    owner = lax.broadcasted_iota(jnp.int32, (128, 1), 0)
    before = jnp.where(
        lax.broadcasted_iota(jnp.int32, (GROUP, GROUP), 0)
        < lax.broadcasted_iota(jnp.int32, (GROUP, GROUP), 1), 1.0, 0.0,
    ).astype(BF16)
    count = jnp.zeros((128, 1), F32)
    for b in range(ROWS // GROUP):
        part = slice(GROUP * b, GROUP * (b + 1))
        target = dest[0:1, part]
        named = jnp.where(target == owner, 1.0, 0.0)
        running = jnp.dot(named.astype(BF16), before, preferred_element_type=F32) + count
        slot = jnp.sum(running * named, axis=0, keepdims=True).astype(jnp.int32)
        count = count + jnp.sum(named, axis=1, keepdims=True)
        position[0:1, part] = jnp.where(slot < 8, 0, PATCH) + target * 8 + slot % 8

    counts = jnp.broadcast_to(count, (128, 128)).astype(BF16)
    expand = jnp.where(
        lax.broadcasted_iota(jnp.int32, (PATCH, 128), 0) // 8
        == lax.broadcasted_iota(jnp.int32, (PATCH, 128), 1), 1.0, 0.0,
    ).astype(BF16)
    filled = jnp.dot(expand, counts, preferred_element_type=F32)
    filled = jnp.concatenate([filled, filled], axis=1)
    slots = (lax.broadcasted_iota(jnp.int32, (PATCH, C), 0) % 8).astype(F32)
    where_to = position[...]
    for patch in range(2):
        index = lax.broadcasted_iota(jnp.int32, (PATCH, 1), 0) + patch * PATCH
        chosen = jnp.where(index == where_to, 1.0, 0.0).astype(BF16)
        moved = jnp.dot(chosen, enriched[...], preferred_element_type=F32)
        outgoing[patch] = to_wire(jnp.where(slots + 8.0 * patch < filled, moved, EMPTY))
        send_some(
            outgoing.at[patch], arrived.at[patch], 0, DEVICES, 1, send_sem.at[patch],
            recv_sem.at[patch],
        )
        keep_own(outgoing.at[patch], arrived.at[patch], recv_sem.at[patch])


def attend(
    exact, arrived, gain, shift, qkv_weight, proj, attended, returned, keys, query_t, value_t,
    mixed_t, send_sem, recv_sem,
):
    rows = from_wire(arrived[...])
    occupied = rows[:, 0:1] < 0.5 * EMPTY
    rows = jnp.where(occupied, rows, 0.0)
    normed = layer_norm(rows, gain[...], shift[...]).astype(BF16)
    qkv = jnp.dot(normed, qkv_weight[...], preferred_element_type=F32).astype(BF16)
    queries = qkv[:, :C]
    keys[...] = qkv[:, C : 2 * C]
    values = jnp.where(occupied, qkv[:, 2 * C :], BF16(0))
    ones = jnp.broadcast_to(jnp.where(occupied, 1.0, 0.0), (PATCH, 128)).astype(BF16).T

    member = jnp.where(
        lax.broadcasted_iota(jnp.int32, (C, 128), 0) // HEAD
        == lax.broadcasted_iota(jnp.int32, (C, 128), 1), 1.0, 0.0,
    ).astype(BF16)

    def largest_square(table):
        wide = table.astype(F32)
        squares = jnp.dot((wide * wide).astype(BF16), member, preferred_element_type=F32)
        return jnp.max(squares, axis=0, keepdims=True)

    bound = jnp.max(
        largest_square(queries) * largest_square(qkv[:, C : 2 * C]), axis=1, keepdims=True
    ) / HEAD
    safe = bound < SAFE_SCORE * SAFE_SCORE

    turned = (queries * BF16(HEAD ** (-0.5))).T
    values_t = values.T
    channel = lax.broadcasted_iota(jnp.int32, (128, 1), 0) // HEAD
    for h in range(HEADS):
        half, inside = h // 8, h % 8
        query_t[h] = jnp.where(channel == inside, turned[128 * half : 128 * (half + 1), :], BF16(0))
        value_t[h, :HEAD] = values_t[HEAD * h : HEAD * (h + 1), :]
        value_t[h, HEAD:] = ones[:HEAD, :]

    penalty = jnp.where(occupied, 0.0, -1e30)

    def head(h, some, columns):
        scores = jnp.dot(some, query_t[h, :, columns], preferred_element_type=F32)
        if exact:
            scores = jnp.where(penalty < 0.0, penalty, scores)
            scores = scores - jnp.max(scores, axis=0, keepdims=True)
        weights = jnp.exp2(scores * LOG2E).astype(BF16)
        products = jnp.dot(value_t[h], weights, preferred_element_type=F32)
        below = products[HEAD : HEAD + 1, :]
        below = jnp.where(below > 0, below, 1.0)
        return (products[:HEAD, :] / below).astype(BF16)

    me = lax.axis_index("space")
    near = BLOCK // 8

    def some_queries(turn, carry):
        block = lax.rem(me // near + turn, PATCH // BLOCK)
        start = pl.multiple_of(block * BLOCK, BLOCK)

        if exact:
            def one_head(t, carry):
                h, offset = t // (BLOCK // 128), t % (BLOCK // 128) * 128
                some = keys[:, pl.ds(pl.multiple_of(h // 8 * 128, 128), 128)]
                mixed_t[h, :, pl.ds(pl.multiple_of(offset, 128), 128)] = head(
                    h, some, pl.ds(pl.multiple_of(start + offset, 128), 128)
                )
                return carry

            lax.fori_loop(0, HEADS * (BLOCK // 128), one_head, 0)
        else:
            for h in range(HEADS):
                some = keys[:, h // 8 * 128 : h // 8 * 128 + 128]
                mixed_t[h] = head(h, some, pl.ds(start, BLOCK))

        mixed = mixed_t[...].reshape(C, BLOCK).T
        result = jnp.dot(mixed, proj[...], preferred_element_type=F32)
        if not exact:
            result = jnp.where(jnp.broadcast_to(safe, (BLOCK, 1)), result, MARK)
        first = pl.multiple_of(block * near, near)
        attended[pl.ds(first, near)] = to_wire(result)

        @pl.when(turn == 0)
        def _():
            keep_own(attended, returned, recv_sem)

        send_some(
            attended, returned, first, near, jnp.where(turn == 0, 1, 0), send_sem, recv_sem
        )
        return carry

    lax.fori_loop(0, PATCH // BLOCK, some_queries, 0)


def transform(rows, attended, gain, shift, fc1, fc2, block_t):
    for b in range(PATCH // GROUP):
        part = slice(GROUP * b, GROUP * (b + 1))
        residual = rows[part] + attended[part]
        normed = layer_norm(residual, gain[...], shift[...]).astype(BF16)
        inner = jnp.dot(normed, fc1[...], preferred_element_type=F32)
        hidden = (0.5 * inner * (1.0 + lax.erf(inner * (0.5 ** 0.5)))).astype(BF16)
        finished = residual + jnp.dot(hidden, fc2[...], preferred_element_type=F32)
        block_t[:, part] = finished.astype(BF16).T


def block_kernel(
    exact,
    feats, brick, row, valid, dest, weight, linear, cpe_gain, cpe_shift, norm1_gain, norm1_shift,
    qkv_far, proj_far, norm2_gain, norm2_shift, fc1_far, fc2_far,
    output, marked,
    enriched, outgoing, arrived, attended, returned, position,
    ext_t, weight_v, weight_t, relative, picked, low, high, qkv_weight, proj, fc1, fc2,
    keys, query_t, value_t, mixed_t, block_t, home_t, chosen, send_sem, recv_sem, load_sem,
):
    loads = [
        pltpu.make_async_copy(far, near, load_sem.at[1 + i])
        for i, (far, near) in enumerate(
            ((qkv_far, qkv_weight), (proj_far, proj), (fc1_far, fc1), (fc2_far, fc2))
        )
    ]
    for load in loads:
        load.start()
    encode(
        feats, brick, row, valid, dest, weight, linear, cpe_gain, cpe_shift,
        enriched, outgoing, arrived, position,
        ext_t, weight_v, weight_t, relative, picked, low, high, send_sem, recv_sem, load_sem,
    )
    index = lax.broadcasted_iota(jnp.int32, (2 * PATCH, 1), 0)
    for b in range(ROWS // GROUP):
        part = slice(GROUP * b, GROUP * (b + 1))
        chosen[:, part] = jnp.where(position[0:1, part] == index, 1.0, 0.0).astype(BF16)
    for load in loads:
        load.wait()

    def own_patch(patch, carry):
        wait_all(outgoing.at[patch], arrived.at[patch], send_sem.at[patch], recv_sem.at[patch])
        attend(
            exact, arrived.at[patch], norm1_gain, norm1_shift, qkv_weight, proj,
            attended.at[patch], returned.at[patch], keys, query_t, value_t, mixed_t,
            send_sem.at[2 + patch], recv_sem.at[2 + patch],
        )
        return carry

    lax.fori_loop(0, 2, own_patch, 0)
    largest = jnp.zeros((1, C), F32)
    for patch in range(2):
        rows = from_wire(outgoing[patch])
        rows = jnp.where(rows[:, 0:1] < 0.5 * EMPTY, rows, 0.0)
        wait_all(
            attended.at[patch], returned.at[patch], send_sem.at[2 + patch], recv_sem.at[2 + patch]
        )
        back = from_wire(returned[patch])
        largest = jnp.maximum(largest, jnp.max(back, axis=0, keepdims=True))
        transform(rows, back, norm2_gain, norm2_shift, fc1, fc2, block_t)
        for b in range(ROWS // GROUP):
            part = slice(GROUP * b, GROUP * (b + 1))
            home = jnp.dot(
                block_t[...], chosen[PATCH * patch : PATCH * (patch + 1), part],
                preferred_element_type=F32,
            )
            if patch == 0:
                home_t[:, part] = home
            else:
                output[part, :] = (home_t[:, part] + home).astype(BF16).T
    marked[...] = jnp.where(largest[:, :1] > 0.1 * MARK, 1, 0)


VMEM = pl.BlockSpec(memory_space=pltpu.VMEM)
FAR = pl.BlockSpec(memory_space=pl.ANY)
WIRE = (2, DEVICES, 16, 128)


def fused(exact, *operands):
    return pl.pallas_call(
        functools.partial(block_kernel, exact),
        out_shape=(
            jax.ShapeDtypeStruct((ROWS, C), BF16),
            jax.ShapeDtypeStruct((1, 1), jnp.int32),
        ),
        in_specs=[FAR if i in (5, 11, 12, 15, 16) else VMEM for i in range(17)],
        out_specs=(VMEM, VMEM),
        scratch_shapes=[
            pltpu.VMEM((ROWS, C), BF16),
            pltpu.VMEM(WIRE, BF16),
            pltpu.VMEM(WIRE, BF16),
            pltpu.VMEM(WIRE, BF16),
            pltpu.VMEM(WIRE, BF16),
            pltpu.VMEM((1, ROWS), jnp.int32),
            pltpu.VMEM((C, 2048), BF16),
            pltpu.VMEM((KOFF, C, C), BF16),
            pltpu.VMEM((C, KOFF * C), BF16),
            pltpu.VMEM((KOFF, ROWS), jnp.int32),
            pltpu.VMEM((KOFF * C, GROUP), BF16),
            pltpu.VMEM((HB * BR, C), BF16),
            pltpu.VMEM((HB * BR, C), BF16),
            pltpu.VMEM((C, 3 * C), BF16),
            pltpu.VMEM((C, C), BF16),
            pltpu.VMEM((C, 4 * C), BF16),
            pltpu.VMEM((4 * C, C), BF16),
            pltpu.VMEM((PATCH, C), BF16),
            pltpu.VMEM((HEADS, 128, PATCH), BF16),
            pltpu.VMEM((HEADS, 2 * HEAD, PATCH), BF16),
            pltpu.VMEM((HEADS, HEAD, BLOCK), BF16),
            pltpu.VMEM((C, PATCH), BF16),
            pltpu.VMEM((C, ROWS), F32),
            pltpu.VMEM((2 * PATCH, ROWS), BF16),
            pltpu.SemaphoreType.DMA((6,)),
            pltpu.SemaphoreType.DMA((6,)),
            pltpu.SemaphoreType.DMA((5,)),
        ],
        compiler_params=pltpu.CompilerParams(
            collective_id=int(exact), has_side_effects=True, vmem_limit_bytes=58 * 2**20
        ),
        name="block_exact" if exact else "block",
    )(*operands)


def per_device(
    feats, nbr_brick, nbr_row, nbr_valid, dest, conv_weight, cpe_linear, cpe_gain, cpe_shift,
    norm1_gain, norm1_shift, qkv_weight, proj_weight, norm2_gain, norm2_shift, fc1_weight,
    fc2_weight,
):
    line = lambda v: v.reshape(1, C)
    operands = (
        feats, nbr_brick, nbr_row, nbr_valid, dest.reshape(1, ROWS), conv_weight, cpe_linear,
        line(cpe_gain), line(cpe_shift), line(norm1_gain), line(norm1_shift), qkv_weight,
        proj_weight, line(norm2_gain), line(norm2_shift), fc1_weight, fc2_weight,
    )
    output, marked = fused(False, *operands)
    return lax.cond(marked[0, 0] == 0, lambda: output, lambda: fused(True, *operands)[0])


def solution(mesh):
    placed = (
        P("space", None), P(None, "space"), P(None, "space"), P(None, "space"), P("space", None),
        P(), P(), P(), P(), P(), P(), P(), P(), P(), P(), P(), P(),
    )
    return jax.shard_map(
        per_device, mesh=mesh, in_specs=placed, out_specs=P("space", None), check_vma=False
    )
```
